32 devices in a mesh: seq: 8 (over y, x, core), hid: 4 (over z).
Axes of the slice: x: 2, y: 2, z: 4, core: 2. Of those that a mesh axis runs over, the one named last changes fastest.
Arguments:
- patches: bfloat16 [3072, 3200], P('seq'), may hold values from -6 to 6
- norm_gain: float32 [3200], replicated, may hold values from 0.5 to 8
- query_weight: bfloat16 [3200, 2048], P(None, 'hid'), may hold values from -0.109375 to 0.109375
- key_weight: bfloat16 [3200, 2048], P(None, 'hid'), may hold values from -0.7424621 to 0.7424621
- value_weight: bfloat16 [3200, 2048], P(None, 'hid'), may hold values from -0.109375 to 0.109375
- out_weight: bfloat16 [2048, 3200], P('hid'), may hold values from -0.125 to 0.125
- layer_scale: float32 [3200], replicated, may hold values from 0.3 to 1.5
- merge_gain: float32 [12800], P('hid'), may hold values from 0.5 to 1.5
- merge_bias: float32 [12800], P('hid'), may hold values from -3 to 3
- proj_weight: bfloat16 [12800, 6144], P('hid', 'seq'), may hold values from -0.0546875 to 0.0546875
- proj_bias: float32 [6144], P('seq'), may hold values from -3 to 3
- text_rows: bfloat16 [128, 6144], P(None, 'seq'), may hold values from -6 to 6
- stream_gain: float32 [6144], P('hid'), may hold values from 0.5 to 1.5
- tile_counts: int32 [2], replicated, may hold values from 1 to 2, as said below
- image_slots: int32 [768], replicated, may hold values from 0 to 895, as said below
- text_slots: int32 [128], replicated, may hold values from 0 to 895, as said below
Outputs:
- stream: bfloat16 [896, 6144], P('seq', 'hid')
- normed: bfloat16 [896, 6144], P('seq', 'hid')
The draws below stay inside these ranges and needn't reach their ends.
Inputs may be any that keep to these rules, and one draw needn't show every extreme that they name: `tile_counts`: the tile counts sum to 3; the largest is exactly 2. `image_slots`: image slots and text slots together name every stream position once; each image's rows lie in order at consecutive positions. `text_slots`: see image_slots; text slots increase.
All inputs are finite; a program needn't handle non-finite values.
Results may differ from the reference program's by a relative error of at most 0.022.
The reference program's roundings to bfloat16 on the way (of `normed_in`, `attended`, `merged_normed` and `image_rows`) count: a program that leaves them out, or rounds other values in their place, can miss the bound.
Values may be sent and summed in bfloat16 or wider, within the bound.
A program may use at most 192 MiB of HBM per device.

```python
import math
import jax
import jax.numpy as jnp
from jax import lax

D = 3200
HEADS = 16
HD = 128
OUT = 6144
SIDE = 32
PATCHES = 3072
TILES = 3
IMAGES = 2
MAXT = 2
IMAGE_TOKENS = 768
MERGED = 12800
TEXT = 128
STREAM = 896


def layout(key):
    base_key = jax.random.fold_in(key, 7)
    order_key, cut_key, split_key = jax.random.split(base_key, 3)
    ranks = jax.random.permutation(order_key, IMAGES).astype(jnp.int32)
    extra_total = TILES - MAXT - (IMAGES - 1)
    inner_cuts = jnp.sort(jax.random.randint(split_key, (IMAGES - 2,), 0, extra_total + 1).astype(jnp.int32))
    edges = jnp.concatenate([jnp.zeros((1,), jnp.int32), inner_cuts, jnp.full((1,), extra_total, jnp.int32)])
    shares = (edges[1:] - edges[:-1]).astype(jnp.int32)
    others = shares[jnp.clip(ranks - 1, 0, IMAGES - 2)]
    counts = jnp.where(ranks == 0, MAXT, 1 + others).astype(jnp.int32)
    cuts = jnp.sort(jax.random.randint(cut_key, (IMAGES,), 0, TEXT + 1).astype(jnp.int32))
    return (counts, cuts)


def draw_tile_counts(key, part):
    counts, cuts = layout(key)
    return counts


def draw_image_slots(key, part):
    counts, cuts = layout(key)
    bounds = jnp.cumsum(counts) * (SIDE * SIDE // 4)
    token_index = jnp.arange(IMAGE_TOKENS, dtype=jnp.int32)
    owner = jnp.sum((token_index[:, None] >= bounds[None, :]).astype(jnp.int32), axis=1)
    return (token_index + cuts[owner]).astype(jnp.int32)


def draw_text_slots(key, part):
    counts, cuts = layout(key)
    starts = jnp.concatenate([jnp.zeros((1,), jnp.int32), jnp.cumsum(counts) * (SIDE * SIDE // 4)]).astype(jnp.int32)
    text_index = jnp.arange(TEXT, dtype=jnp.int32)
    segment = jnp.sum((text_index[:, None] >= cuts[None, :]).astype(jnp.int32), axis=1)
    return (text_index + starts[segment]).astype(jnp.int32)


def draw_norm_gain(key, part):
    return jax.random.uniform(key, (D,), jnp.float32, 0.7, 1.3)


def draw_key_weight(key, part):
    shift_key, entry_key = jax.random.split(jax.random.fold_in(key, 11))
    strengths = jnp.array([1.0, 2.5, 4.5, 7.0], jnp.float32)
    offset = jax.random.randint(shift_key, (), 0, 4).astype(jnp.int32)
    head_index = jnp.arange(HEADS, dtype=jnp.int32)
    factor = jnp.repeat(strengths[(head_index + offset) % 4], HD)
    entries = jnp.clip(jax.random.normal(entry_key, (D, HEADS * HD), jnp.float32), -6.0, 6.0)
    return (entries * D ** (-0.5) * factor[None, :]).astype(jnp.bfloat16)


def level_of(rng, dims, cuts, least, largest):
    def one(dim, blocks):
        steps = jax.random.uniform(jax.random.fold_in(jax.random.fold_in(rng, 6), dim), (blocks,), jnp.float32, least / len(cuts), largest / len(cuts))
        return jnp.repeat(jnp.exp(steps), dims[dim] // blocks).reshape((-1,) + (1,) * (len(dims) - dim - 1))

    factor_of = one(*cuts[0])
    for cut in cuts[1:]:
        factor_of = factor_of * one(*cut)
    return factor_of


def centred(own_key, shape, scale, reach, cuts=(), kind=jnp.bfloat16):
    gain = level_of(own_key, shape, cuts, -0.22, 0.18) if cuts else 1.0
    values = jax.random.normal(own_key, shape, jnp.float32) * scale * gain
    return jnp.minimum(jnp.maximum(values, -reach), reach).astype(kind)


def setup_inputs(seed: int = 0) -> dict:
    arg_keys = jax.random.split(jax.random.key(seed), 17)
    return {
        "patches": centred(arg_keys[0], (PATCHES, D), 1.0, 6.0, ((0, 8),)),
        "norm_gain": draw_norm_gain(jax.random.fold_in(arg_keys[16], 71), 0),
        "query_weight": centred(arg_keys[2], (D, HEADS * HD), D ** -0.5, 0.109375, ((1, 4),)),
        "key_weight": draw_key_weight(jax.random.fold_in(arg_keys[16], 71), 0),
        "value_weight": centred(arg_keys[4], (D, HEADS * HD), D ** -0.5, 0.109375, ((1, 4),)),
        "out_weight": centred(arg_keys[5], (HEADS * HD, D), (HEADS * HD) ** -0.5, 0.125, ((0, 4),)),
        "layer_scale": jnp.clip(jnp.exp(jax.random.uniform(arg_keys[6], (D,), jnp.float32, math.log(0.3), math.log(1.5))), 0.3, 1.5),
        "merge_gain": jnp.clip(1.0 + 0.1 * jax.random.normal(arg_keys[7], (MERGED,), jnp.float32), 0.5, 1.5),
        "merge_bias": centred(arg_keys[8], (MERGED,), 0.5, 3.0, ((0, 4),), jnp.float32),
        "proj_weight": centred(arg_keys[9], (MERGED, OUT), MERGED ** -0.5, 0.0546875, ((0, 4), (1, 8))),
        "proj_bias": centred(arg_keys[10], (OUT,), 0.5, 3.0, ((0, 8),), jnp.float32),
        "text_rows": centred(arg_keys[11], (TEXT, OUT), 1.0, 6.0, ((1, 8),)),
        "stream_gain": jnp.clip(1.0 + 0.1 * jax.random.normal(arg_keys[12], (OUT,), jnp.float32), 0.5, 1.5),
        "tile_counts": draw_tile_counts(jax.random.fold_in(arg_keys[16], 71), 0),
        "image_slots": draw_image_slots(jax.random.fold_in(arg_keys[16], 71), 0),
        "text_slots": draw_text_slots(jax.random.fold_in(arg_keys[16], 71), 0),
    }


def image_of(index_rows, tile_counts):
    bounds = jnp.cumsum(tile_counts) * (SIDE * SIDE)
    return lax.optimization_barrier(jnp.sum((index_rows[:, None] >= bounds[None, :]).astype(jnp.int32), axis=1))

def shuffle_rows(values):
    row_count, width = values.shape
    grouped = values.reshape(row_count // (2 * SIDE), 2, SIDE // 2, 2, width)
    return grouped.transpose(0, 2, 4, 1, 3).reshape(row_count // 4, 4 * width)

def reference(patches, norm_gain, query_weight, key_weight, value_weight, out_weight, layer_scale, merge_gain, merge_bias, proj_weight, proj_bias, text_rows, stream_gain, tile_counts, image_slots, text_slots):
    tokens_f = patches.astype(jnp.float32)
    normed_in = (tokens_f * lax.rsqrt(lax.optimization_barrier(jnp.mean(tokens_f * tokens_f, -1, keepdims=True)) + 1e-06) * norm_gain).astype(jnp.bfloat16)
    queries = (jnp.dot(normed_in, query_weight, preferred_element_type=jnp.float32) * HD ** (-0.5)).astype(jnp.bfloat16)
    key_rows = jnp.dot(normed_in, key_weight, preferred_element_type=jnp.float32).astype(jnp.bfloat16)
    value_rows = jnp.dot(normed_in, value_weight, preferred_element_type=jnp.float32).astype(jnp.bfloat16)
    image_ids = image_of(jnp.arange(PATCHES, dtype=jnp.int32), tile_counts)
    same_image = image_ids[:, None] == image_ids[None, :]
    query_heads = queries.reshape(PATCHES, HEADS, HD).transpose(1, 0, 2)
    key_heads = key_rows.reshape(PATCHES, HEADS, HD).transpose(1, 0, 2)
    value_heads = value_rows.reshape(PATCHES, HEADS, HD).transpose(1, 0, 2)

    def one_head(operands):
        query_one, key_one, value_one = operands
        scores = jnp.dot(query_one, key_one.T, preferred_element_type=jnp.float32)
        scores = jnp.where(same_image, scores, jnp.float32(-1e+30))
        row_max = lax.optimization_barrier(jnp.max(scores, axis=1, keepdims=True))
        weights = jnp.where(same_image, jnp.exp(scores - row_max), jnp.float32(0.0))
        totals = lax.optimization_barrier(jnp.sum(weights, axis=1, keepdims=True))
        summed = jnp.dot(weights.astype(jnp.bfloat16), value_one, preferred_element_type=jnp.float32)
        return (summed / totals).astype(jnp.bfloat16)
    attended = lax.map(one_head, (query_heads, key_heads, value_heads))
    attended = attended.transpose(1, 0, 2).reshape(PATCHES, HEADS * HD)
    branch = jnp.dot(attended, out_weight, preferred_element_type=jnp.float32)
    residual = tokens_f + layer_scale * branch
    merged = shuffle_rows(residual)
    mean_row = lax.optimization_barrier(jnp.mean(merged, -1, keepdims=True))
    var_row = lax.optimization_barrier(jnp.mean(merged * merged, -1, keepdims=True)) - mean_row * mean_row
    merged_normed = ((merged - mean_row) * lax.rsqrt(var_row + 1e-05) * merge_gain + merge_bias).astype(jnp.bfloat16)
    projected = jnp.dot(merged_normed, proj_weight, preferred_element_type=jnp.float32) + proj_bias
    image_rows = jax.nn.gelu(projected, approximate=False).astype(jnp.bfloat16)
    stream = jnp.zeros((STREAM, OUT), jnp.bfloat16).at[image_slots].set(image_rows).at[text_slots].set(text_rows)
    stream_f = stream.astype(jnp.float32)
    normed = (stream_f * lax.rsqrt(lax.optimization_barrier(jnp.mean(stream_f * stream_f, -1, keepdims=True)) + 1e-05) * stream_gain).astype(jnp.bfloat16)
    return (stream, normed)
```

```python
import functools

import jax
import jax.numpy as jnp
from jax import lax
from jax.experimental import pallas as pl
from jax.experimental.pallas import tpu as pltpu
from jax.sharding import PartitionSpec as P

HD = 128
SIDE = 32
TILE = SIDE * SIDE
BLOCK = 128
MESH = pl.DeviceIdType.MESH
F32 = jnp.float32
BF16 = jnp.bfloat16
VMEM = pl.BlockSpec(memory_space=pltpu.VMEM)
LIMIT = 50 * 1024 * 1024


def params(number):
    return pltpu.CompilerParams(
        collective_id=number, has_side_effects=True, vmem_limit_bytes=LIMIT
    )


def greet(peers):
    barrier = pltpu.get_barrier_semaphore()
    for peer in peers:
        pl.semaphore_signal(barrier, inc=1, device_id=peer, device_id_type=MESH)
    pl.semaphore_wait(barrier, len(peers))


def remote(src, dst, send_sem, recv_sem, peer):
    return pltpu.make_async_remote_copy(
        src_ref=src,
        dst_ref=dst,
        send_sem=send_sem,
        recv_sem=recv_sem,
        device_id=peer,
        device_id_type=MESH,
    )


def head_cols(index):
    return pl.ds(pl.multiple_of(index * HD, HD), HD)


def exchange_kernel(L, G, q_ref, k_ref, v_ref, qo, ko, vo, send1, recv1, send2, recv2):
    s = lax.axis_index("seq")
    c, k = s // G, s % G
    places = [(c + t) % L for t in range(1, L)]
    mates = [(k + t) % G for t in range(1, G)]
    greet([{"seq": o * G + k} for o in places] + [{"seq": c * G + m} for m in mates])
    ins, outs = (k_ref, v_ref, q_ref), (ko, vo, qo)
    sent = []
    for t, o in enumerate(places):
        for a in range(3):
            copy = remote(
                ins[a].at[:, head_cols(o)], outs[a].at[s], send1.at[t, a], recv1.at[c, a],
                {"seq": o * G + k},
            )
            copy.start()
            sent.append(copy)
    own = head_cols(c)
    for a in range(3):
        outs[a][s] = ins[a][:, own]

    def share(t, slot, home):
        for u, m in enumerate(mates):
            for a in range(2):
                copy = remote(
                    outs[a].at[slot], outs[a].at[slot], send2.at[t, u, a], recv2.at[home, k, a],
                    {"seq": c * G + m},
                )
                copy.start()
                sent.append(copy)

    share(0, s, c)
    for t in range(1, L):
        o = (c - t + L) % L
        for a in range(3):
            remote(
                outs[a].at[o * G + k], outs[a].at[o * G + k], send1.at[0, a], recv1.at[o, a],
                {"seq": o * G + k},
            ).wait_recv()
        share(t, o * G + k, o)
    for m in mates:
        for t in range(L):
            o = (c + t) % L
            for a in range(2):
                remote(
                    outs[a].at[o * G + m], outs[a].at[o * G + m], send2.at[0, 0, a],
                    recv2.at[o, m, a], {"seq": c * G + m},
                ).wait_recv()
    for copy in sent:
        copy.wait_send()


def exchange(q, k, v, S, L):
    G = S // L
    rows = q.shape[0]
    shape = jax.ShapeDtypeStruct((S, rows, HD), BF16)
    return pl.pallas_call(
        functools.partial(exchange_kernel, L, G),
        out_shape=(shape,) * 3,
        in_specs=[VMEM] * 3,
        out_specs=(VMEM,) * 3,
        scratch_shapes=[
            pltpu.SemaphoreType.DMA((L, 3)),
            pltpu.SemaphoreType.DMA((L, 3)),
            pltpu.SemaphoreType.DMA((L, G, 2)),
            pltpu.SemaphoreType.DMA((L, G, 2)),
        ],
        compiler_params=params(0),
        name="exchange_heads",
    )(q, k, v)


def attend_kernel(G, rows, lo, hi, place, q_ref, k_ref, v_ref, out_ref):
    first = (pl.program_id(0) * G + place[0]) * rows + pl.program_id(1) * BLOCK
    tile = lax.div(first, TILE)
    q = q_ref[0]

    def step(t, carry):
        top, total, acc = carry
        span = pl.ds(pl.multiple_of(t * TILE, TILE), TILE)
        scores = lax.dot_general(
            q, k_ref[span, :], (((1,), (1,)), ((), ())), preferred_element_type=F32
        )
        new_top = jnp.maximum(top, jnp.max(scores, axis=1, keepdims=True))
        factor = jnp.exp(top - new_top)
        weights = jnp.exp(scores - new_top)
        total = total * factor + jnp.sum(weights, axis=1, keepdims=True)
        acc = acc * factor + jnp.dot(
            weights.astype(BF16), v_ref[span, :], preferred_element_type=F32
        )
        return new_top, total, acc

    start = (
        jnp.full((BLOCK, 1), -1e30, F32),
        jnp.zeros((BLOCK, 1), F32),
        jnp.zeros((BLOCK, HD), F32),
    )
    top, total, acc = lax.fori_loop(lo[tile], hi[tile], step, start)
    out_ref[0] = (acc / total).astype(BF16)


def attend(q, k, v, lo, hi, place, S, L):
    G = S // L
    rows = q.shape[1]
    return pl.pallas_call(
        functools.partial(attend_kernel, G, rows),
        out_shape=jax.ShapeDtypeStruct((L, rows, HD), BF16),
        grid_spec=pltpu.PrefetchScalarGridSpec(
            num_scalar_prefetch=3,
            grid=(L, rows // BLOCK),
            in_specs=[
                pl.BlockSpec((1, BLOCK, HD), lambda a, b, lo, hi, p: (a * G + p[0], b, 0)),
                VMEM,
                VMEM,
            ],
            out_specs=pl.BlockSpec((1, BLOCK, HD), lambda a, b, lo, hi, p: (a, b, 0)),
        ),
        compiler_params=pltpu.CompilerParams(vmem_limit_bytes=LIMIT),
        name="attend",
    )(lo, hi, place, q, k.reshape(S * rows, HD), v.reshape(S * rows, HD))


def spread_kernel(L, G, H, a_ref, out, send, recv):
    s, h = lax.axis_index("seq"), lax.axis_index("hid")
    c, k = s // G, s % G
    peers = [
        ((c + dc) % L, (h + dh) % H) for dh in range(H) for dc in range(L) if dc or dh
    ]
    ids = [{"seq": o * G + k, "hid": z} for o, z in peers]
    greet(ids)
    mine = h * L + c
    sent = []
    for t, (o, z) in enumerate(peers):
        copy = remote(
            a_ref.at[o], out.at[:, head_cols(mine)], send.at[t], recv.at[mine], ids[t]
        )
        copy.start()
        sent.append(copy)
    out[:, head_cols(mine)] = a_ref[c]
    for t, (o, z) in enumerate(peers):
        source = z * L + o
        remote(
            a_ref.at[o], out.at[:, head_cols(source)], send.at[t], recv.at[source], ids[t]
        ).wait_recv()
    for copy in sent:
        copy.wait_send()


def spread(a, S, L, H):
    rows = a.shape[1]
    return pl.pallas_call(
        functools.partial(spread_kernel, L, S // L, H),
        out_shape=jax.ShapeDtypeStruct((rows, H * L * HD), BF16),
        in_specs=[VMEM],
        out_specs=VMEM,
        scratch_shapes=[
            pltpu.SemaphoreType.DMA((H * L,)),
            pltpu.SemaphoreType.DMA((H * L,)),
        ],
        compiler_params=params(1),
        name="spread_attended",
    )(a)


def merge_kernel(
    L, G, H, a_ref, w_ref, x_ref, ls_ref, gain_ref, bias_ref, out,
    res, stats, lanes, place, ssend, srecv, send1, recv1, send2, recv2,
):
    s, h = lax.axis_index("seq"), lax.axis_index("hid")
    c, k = s // G, s % G
    planes = [(h + t) % H for t in range(1, H)]
    places = [(c + t) % L for t in range(1, L)]
    mates = [(k + t) % G for t in range(1, G)]
    greet(
        [{"hid": z} for z in planes]
        + [{"seq": o * G + k} for o in places]
        + [{"seq": c * G + m} for m in mates]
    )
    rows, width = x_ref.shape
    sub = BLOCK // 4
    full = width // HD
    for b in range(rows // BLOCK):
        span = slice(b * BLOCK, (b + 1) * BLOCK)
        branch = jnp.dot(a_ref[span, :], w_ref[...], preferred_element_type=F32)
        value = x_ref[span, :].astype(F32) + ls_ref[...] * branch
        res[span, :] = value
        one = jnp.sum(value, axis=1, keepdims=True)
        two = jnp.sum(value * value, axis=1, keepdims=True)
        for n, column in ((0, one), (1, two)):
            summed = sum(column[q * sub : (q + 1) * sub] for q in range(4))
            stats[h, n, b * sub : (b + 1) * sub, :] = jnp.broadcast_to(summed, (sub, HD))
    sent = []
    for t, z in enumerate(planes):
        copy = remote(stats.at[h], stats.at[h], ssend.at[t], srecv.at[h], {"hid": z})
        copy.start()
        sent.append(copy)
    lanes[...] = jnp.zeros_like(lanes)
    row = lax.broadcasted_iota(jnp.int32, (4 * HD, 4 * HD), 0)
    col = lax.broadcasted_iota(jnp.int32, (4 * HD, 4 * HD), 1)
    place[...] = jnp.where(col == 4 * (row % HD) + lax.div(row, HD), 1.0, 0.0).astype(BF16)
    for t, z in enumerate(planes):
        remote(stats.at[z], stats.at[z], ssend.at[t], srecv.at[z], {"hid": z}).wait_recv()
    total = stats[0]
    for z in range(1, H):
        total = total + stats[z]
    total = total * (1.0 / (4 * width * H))
    mean = total[0]
    scale = lax.rsqrt(total[1] - mean * mean + 1e-05)
    for b in range(rows // BLOCK):
        part = slice(b * sub, (b + 1) * sub)
        mean_b, scale_b = mean[part, :1], scale[part, :1]
        for q in range(4):
            start = b * BLOCK + q * sub
            value = (res[start : start + sub, :] - mean_b) * scale_b
            value = (value * gain_ref[q : q + 1, :] + bias_ref[q : q + 1, :]).astype(BF16)
            for j in range(full):
                lanes[part, (4 * j + q) * HD : (4 * j + q + 1) * HD] = value[:, j * HD : (j + 1) * HD]
            if width % HD:
                at = (4 * full + q) * HD
                lanes[part, at : at + width % HD] = value[:, full * HD :]
    for j in range(full):
        cols = slice(4 * j * HD, 4 * (j + 1) * HD)
        out[s, :, cols] = jnp.dot(
            lanes[:, cols], place[...], preferred_element_type=F32
        ).astype(BF16)
    if width % HD:
        cols = slice(4 * full * HD, 4 * (full + 1) * HD)
        left = 4 * (width % HD)
        last = jnp.dot(lanes[:, cols], place[...], preferred_element_type=F32)
        out[s, :, 4 * full * HD :] = last[:, :left].astype(BF16)
    for t, o in enumerate(places):
        copy = remote(out.at[s], out.at[s], send1.at[t], recv1.at[c], {"seq": o * G + k})
        copy.start()
        sent.append(copy)

    def share(t, slot, home):
        for u, m in enumerate(mates):
            copy = remote(
                out.at[slot], out.at[slot], send2.at[t, u], recv2.at[home, k], {"seq": c * G + m}
            )
            copy.start()
            sent.append(copy)

    share(0, s, c)
    for t in range(1, L):
        o = (c - t + L) % L
        slot = o * G + k
        remote(out.at[slot], out.at[slot], send1.at[0], recv1.at[o], {"seq": slot}).wait_recv()
        share(t, slot, o)
    for m in mates:
        for t in range(L):
            o = (c + t) % L
            slot = o * G + m
            remote(
                out.at[slot], out.at[slot], send2.at[0, 0], recv2.at[o, m], {"seq": c * G + m}
            ).wait_recv()
    for copy in sent:
        copy.wait_send()


def merge(a, w, x, ls, gain, bias, S, L, H):
    G = S // L
    rows, width = x.shape
    return pl.pallas_call(
        functools.partial(merge_kernel, L, G, H),
        out_shape=jax.ShapeDtypeStruct((S, rows // 4, 4 * width), BF16),
        in_specs=[VMEM] * 6,
        out_specs=VMEM,
        scratch_shapes=[
            pltpu.VMEM((rows, width), F32),
            pltpu.VMEM((H, 2, rows // 4, HD), F32),
            pltpu.VMEM((rows // 4, 4 * HD * pl.cdiv(width, HD)), BF16),
            pltpu.VMEM((4 * HD, 4 * HD), BF16),
            pltpu.SemaphoreType.DMA((H,)),
            pltpu.SemaphoreType.DMA((H,)),
            pltpu.SemaphoreType.DMA((L,)),
            pltpu.SemaphoreType.DMA((L,)),
            pltpu.SemaphoreType.DMA((L, G)),
            pltpu.SemaphoreType.DMA((L, G)),
        ],
        compiler_params=params(2),
        name="merge_rows",
    )(a, w, x, ls, gain, bias)


def finish_kernel(
    g, H, p_ref, bias_ref, text_ref, mask_ref, gain_ref, stream, normed,
    parts, rows_out, rows_in, squares, send1, recv1, send2, recv2, send3, recv3,
):
    s, h = lax.axis_index("seq"), lax.axis_index("hid")
    c, k = s // g, s % g
    planes = [(h + t) % H for t in range(1, H)]
    off = c != h
    barrier = pltpu.get_barrier_semaphore()
    for z in planes:
        pl.semaphore_signal(barrier, inc=1, device_id={"hid": z}, device_id_type=MESH)
    for t in range(g):
        j = (k + t) % g
        partner = {"seq": g * h + j, "hid": c}
        if t:
            pl.semaphore_signal(barrier, inc=1, device_id=partner, device_id_type=MESH)
        else:
            @pl.when(off)
            def _():
                pl.semaphore_signal(barrier, inc=1, device_id=partner, device_id_type=MESH)
    pl.semaphore_wait(barrier, len(planes) + g - 1 + off.astype(jnp.int32))

    sent = []
    for t, z in enumerate(planes):
        copy = remote(p_ref.at[z], parts.at[h], send1.at[t], recv1.at[h], {"hid": z})
        copy.start()
        sent.append(copy)
    for t, z in enumerate(planes):
        remote(p_ref.at[z], parts.at[z], send1.at[t], recv1.at[z], {"hid": z}).wait_recv()
    part_rows = stream.shape[0]
    width = bias_ref.shape[1]
    for j in range(g):
        span = slice(j * part_rows, (j + 1) * part_rows)
        value = p_ref[h, span, :].astype(F32)
        for z in planes:
            value = value + parts[z, span, :].astype(F32)
        value = value + bias_ref[...]
        value = value * (lax.erf(value * F32(0.7071067811865476)) + 1.0) * 0.5
        rows_out[j] = jnp.where(
            mask_ref[span, :1] > 0.5, value, text_ref[span, :].astype(F32)
        ).astype(BF16)
    for t in range(g):
        j = (k + t) % g
        partner = {"seq": g * h + j, "hid": c}
        copy = remote(rows_out.at[j], rows_in.at[k], send2.at[t], recv2.at[k], partner)
        if t:
            copy.start()
            sent.append(copy)
        else:
            pl.when(off)(copy.start)

            @pl.when(jnp.logical_not(off))
            def _():
                rows_in[k] = rows_out[k]

    for t in range(g):
        j = (k + t) % g
        partner = {"seq": g * h + j, "hid": c}
        copy = remote(rows_out.at[j], rows_in.at[j], send2.at[t], recv2.at[j], partner)
        if t:
            copy.wait_recv()
        else:
            @pl.when(off)
            def _():
                copy.wait_recv()
                copy.wait_send()
    square = jnp.zeros((part_rows, 1), F32)
    for j in range(g):
        value = rows_in[j]
        stream[:, j * width : (j + 1) * width] = value
        value = value.astype(F32)
        square = square + jnp.sum(value * value, axis=1, keepdims=True)
    squares[h] = jnp.broadcast_to(square, squares.shape[1:])
    for t, z in enumerate(planes):
        copy = remote(squares.at[h], squares.at[h], send3.at[t], recv3.at[h], {"hid": z})
        copy.start()
        sent.append(copy)
    for t, z in enumerate(planes):
        remote(squares.at[z], squares.at[z], send3.at[t], recv3.at[z], {"hid": z}).wait_recv()
    total = squares[0]
    for z in range(1, H):
        total = total + squares[z]
    scale = lax.rsqrt(total * (1.0 / (g * width * H)) + 1e-05)[:, :1]
    normed[...] = (stream[...].astype(F32) * scale * gain_ref[...]).astype(BF16)
    for copy in sent:
        copy.wait_send()


def finish(placed, bias, text, mask, gain, S, H):
    g = S // H
    width = placed.shape[-1]
    part_rows = placed.shape[1] // g
    shape = jax.ShapeDtypeStruct((part_rows, g * width), BF16)
    return pl.pallas_call(
        functools.partial(finish_kernel, g, H),
        out_shape=(shape, shape),
        in_specs=[VMEM] * 5,
        out_specs=(VMEM, VMEM),
        scratch_shapes=[
            pltpu.VMEM((H, g * part_rows, width), BF16),
            pltpu.VMEM((g, part_rows, width), BF16),
            pltpu.VMEM((g, part_rows, width), BF16),
            pltpu.VMEM((H, part_rows, HD), F32),
            pltpu.SemaphoreType.DMA((H,)),
            pltpu.SemaphoreType.DMA((H,)),
            pltpu.SemaphoreType.DMA((g,)),
            pltpu.SemaphoreType.DMA((g,)),
            pltpu.SemaphoreType.DMA((H,)),
            pltpu.SemaphoreType.DMA((H,)),
        ],
        compiler_params=params(3),
        name="finish_rows",
    )(placed, bias, text, mask, gain)


def grouping():
    new = jnp.arange(BLOCK, dtype=jnp.int32)
    half = SIDE // 2
    quarter = BLOCK // 4
    spot, rest = new // quarter, new % quarter
    pair, c2 = rest // half, rest % half
    old = (2 * pair + spot // 2) * SIDE + 2 * c2 + spot % 2
    return (old[:, None] == new[None, :]).astype(BF16)


def per_device(
    patches,
    norm_gain,
    query_weight,
    key_weight,
    value_weight,
    out_weight,
    layer_scale,
    merge_gain,
    merge_bias,
    proj_weight,
    proj_bias,
    text_rows,
    stream_gain,
    tile_counts,
    image_slots,
    text_slots,
):
    S, H = lax.axis_size("seq"), lax.axis_size("hid")
    s, h = lax.axis_index("seq"), lax.axis_index("hid")
    rows, depth = patches.shape
    L = query_weight.shape[1] // HD
    G = S // L
    quarter = depth // H

    head_rows = out_weight.shape[0]
    piece = head_rows // S
    own_rows = lax.dynamic_slice_in_dim(out_weight, s * piece, piece, 0)
    own_rows = own_rows.reshape(piece, H, quarter).transpose(1, 0, 2)
    own_cols = lax.all_to_all(own_rows, "hid", split_axis=0, concat_axis=0, tiled=True)
    all_cols = lax.all_gather(own_cols, "seq", axis=0, tiled=False)
    out_cols = all_cols.transpose(1, 0, 2, 3).reshape(H * head_rows, quarter)

    grouped = jnp.einsum(
        "ij,bjd->bid", grouping(), patches.reshape(rows // BLOCK, BLOCK, depth),
        preferred_element_type=F32,
    ).astype(BF16).reshape(rows, depth)
    tokens_f = grouped.astype(F32)
    normed_in = (
        tokens_f * lax.rsqrt(jnp.mean(tokens_f * tokens_f, -1, keepdims=True) + 1e-06) * norm_gain
    ).astype(BF16)
    queries = (
        jnp.dot(normed_in, query_weight, preferred_element_type=F32) * HD ** (-0.5)
    ).astype(BF16)
    key_rows = jnp.dot(normed_in, key_weight, preferred_element_type=F32).astype(BF16)
    value_rows = jnp.dot(normed_in, value_weight, preferred_element_type=F32).astype(BF16)

    q_all, k_all, v_all = exchange(queries, key_rows, value_rows, S, L)
    tiles = S * rows // TILE
    ends = jnp.cumsum(tile_counts).astype(jnp.int32)
    tile = jnp.arange(tiles, dtype=jnp.int32)
    after = tile[:, None] >= ends[None, :]
    lo = jnp.max(jnp.where(after, ends[None, :], 0), axis=1).astype(jnp.int32)
    hi = jnp.min(jnp.where(after, tiles, ends[None, :]), axis=1).astype(jnp.int32)
    place = (s % G).astype(jnp.int32).reshape(1)
    heads = attend(q_all, k_all, v_all, lo, hi, place, S, L)
    attended = spread(heads, S, L, H)

    own_tokens = lax.dynamic_slice_in_dim(grouped, h * quarter, quarter, 1)
    own_scale = lax.dynamic_slice_in_dim(layer_scale, h * quarter, quarter, 0)
    merged_normed = merge(
        attended,
        out_cols,
        own_tokens,
        own_scale.reshape(1, quarter),
        merge_gain.reshape(quarter, 4).T,
        merge_bias.reshape(quarter, 4).T,
        S,
        L,
        H,
    )
    partial = jnp.dot(
        merged_normed.reshape(S * rows // 4, 4 * quarter), proj_weight, preferred_element_type=F32
    ).astype(BF16)
    stream_size = image_slots.shape[0] + text_slots.shape[0]
    positions = jnp.arange(stream_size, dtype=jnp.int32)
    chosen = (positions[:, None] == image_slots[None, :]).astype(BF16)
    placed = jnp.dot(chosen, partial, preferred_element_type=F32).astype(BF16)
    share = stream_size // H
    width = partial.shape[1]
    own_positions = h * share + jnp.arange(share, dtype=jnp.int32)
    is_text = own_positions[:, None] == text_slots[None, :]
    text = jnp.dot(is_text.astype(BF16), text_rows, preferred_element_type=F32).astype(BF16)
    is_image = jnp.where(jnp.any(is_text, axis=1, keepdims=True), 0.0, 1.0)
    mask = jnp.broadcast_to(is_image.astype(F32), (share, HD))
    return finish(
        placed.reshape(H, share, width),
        proj_bias.reshape(1, width),
        text,
        mask,
        stream_gain.reshape(1, stream_gain.shape[0]),
        S,
        H,
    )


def solution(mesh):
    return jax.shard_map(
        per_device,
        mesh=mesh,
        in_specs=(
            P("seq", None),
            P(),
            P(None, "hid"),
            P(None, "hid"),
            P(None, "hid"),
            P("hid", None),
            P(),
            P("hid"),
            P("hid"),
            P("hid", "seq"),
            P("seq"),
            P(None, "seq"),
            P("hid"),
            P(),
            P(),
            P(),
        ),
        out_specs=(P("seq", "hid"), P("seq", "hid")),
        check_vma=False,
    )
```

```python
import functools

import jax
import jax.numpy as jnp
from jax import lax
from jax.experimental import pallas as pl
from jax.experimental.pallas import tpu as pltpu
from jax.sharding import PartitionSpec as P

HD = 128
SIDE = 32
TILE = SIDE * SIDE
BLOCK = 128
MESH = pl.DeviceIdType.MESH
F32 = jnp.float32
BF16 = jnp.bfloat16
VMEM = pl.BlockSpec(memory_space=pltpu.VMEM)
LIMIT = 50 * 1024 * 1024


def params(number):
    return pltpu.CompilerParams(
        collective_id=number, has_side_effects=True, vmem_limit_bytes=LIMIT
    )


def greet(peers):
    barrier = pltpu.get_barrier_semaphore()
    for peer in peers:
        pl.semaphore_signal(barrier, inc=1, device_id=peer, device_id_type=MESH)
    pl.semaphore_wait(barrier, len(peers))


def remote(src, dst, send_sem, recv_sem, peer):
    return pltpu.make_async_remote_copy(
        src_ref=src,
        dst_ref=dst,
        send_sem=send_sem,
        recv_sem=recv_sem,
        device_id=peer,
        device_id_type=MESH,
    )


def head_cols(index):
    return pl.ds(pl.multiple_of(index * HD, HD), HD)


def exchange_kernel(
    L, G, H, q_ref, k_ref, v_ref, w_ref, qo, ko, vo, wo, send1, recv1, send2, recv2, send3, recv3
):
    s, h = lax.axis_index("seq"), lax.axis_index("hid")
    c, k = s // G, s % G
    planes = [(h + t) % H for t in range(1, H)]
    places = [(c + t) % L for t in range(1, L)]
    mates = [(k + t) % G for t in range(1, G)]
    greet(
        [{"hid": z} for z in planes]
        + [{"seq": o * G + k} for o in places]
        + [{"seq": c * G + m} for m in mates]
    )
    ins, outs = (k_ref, v_ref, q_ref), (ko, vo, qo)
    sent = []
    for t, o in enumerate(places):
        for a in range(3):
            copy = remote(
                ins[a].at[:, head_cols(o)], outs[a].at[s], send1.at[t, a], recv1.at[c, a],
                {"seq": o * G + k},
            )
            copy.start()
            sent.append(copy)
    for t, z in enumerate(planes):
        copy = remote(w_ref.at[z], wo.at[h], send3.at[t], recv3.at[h], {"hid": z})
        copy.start()
        sent.append(copy)
    wo[h] = w_ref[h]
    own = head_cols(c)
    for a in range(3):
        outs[a][s] = ins[a][:, own]

    def share(t, slot, home):
        for u, m in enumerate(mates):
            for a in range(2):
                copy = remote(
                    outs[a].at[slot], outs[a].at[slot], send2.at[t, u, a], recv2.at[home, k, a],
                    {"seq": c * G + m},
                )
                copy.start()
                sent.append(copy)

    share(0, s, c)
    for t in range(1, L):
        o = (c - t + L) % L
        for a in range(3):
            remote(
                outs[a].at[o * G + k], outs[a].at[o * G + k], send1.at[0, a], recv1.at[o, a],
                {"seq": o * G + k},
            ).wait_recv()
        share(t, o * G + k, o)
    for m in mates:
        for t in range(L):
            o = (c + t) % L
            for a in range(2):
                remote(
                    outs[a].at[o * G + m], outs[a].at[o * G + m], send2.at[0, 0, a],
                    recv2.at[o, m, a], {"seq": c * G + m},
                ).wait_recv()
    for t, z in enumerate(planes):
        remote(w_ref.at[z], wo.at[z], send3.at[t], recv3.at[z], {"hid": z}).wait_recv()
    for copy in sent:
        copy.wait_send()


def exchange(q, k, v, w, S, L, H):
    G = S // L
    rows = q.shape[0]
    shape = jax.ShapeDtypeStruct((S, rows, HD), BF16)
    return pl.pallas_call(
        functools.partial(exchange_kernel, L, G, H),
        out_shape=(shape,) * 3 + (jax.ShapeDtypeStruct(w.shape, w.dtype),),
        in_specs=[VMEM] * 4,
        out_specs=(VMEM,) * 4,
        scratch_shapes=[
            pltpu.SemaphoreType.DMA((L, 3)),
            pltpu.SemaphoreType.DMA((L, 3)),
            pltpu.SemaphoreType.DMA((L, G, 2)),
            pltpu.SemaphoreType.DMA((L, G, 2)),
            pltpu.SemaphoreType.DMA((H,)),
            pltpu.SemaphoreType.DMA((H,)),
        ],
        compiler_params=params(0),
        name="exchange_heads",
    )(q, k, v, w)


def attend_kernel(G, rows, lo, hi, place, q_ref, k_ref, v_ref, out_ref):
    first = (pl.program_id(0) * G + place[0]) * rows + pl.program_id(1) * BLOCK
    tile = lax.div(first, TILE)
    q = q_ref[0]

    def step(t, carry):
        top, total, acc = carry
        span = pl.ds(pl.multiple_of(t * TILE, TILE), TILE)
        scores = lax.dot_general(
            q, k_ref[span, :], (((1,), (1,)), ((), ())), preferred_element_type=F32
        )
        new_top = jnp.maximum(top, jnp.max(scores, axis=1, keepdims=True))
        factor = jnp.exp(top - new_top)
        weights = jnp.exp(scores - new_top)
        total = total * factor + jnp.sum(weights, axis=1, keepdims=True)
        acc = acc * factor + jnp.dot(
            weights.astype(BF16), v_ref[span, :], preferred_element_type=F32
        )
        return new_top, total, acc

    start = (
        jnp.full((BLOCK, 1), -1e30, F32),
        jnp.zeros((BLOCK, 1), F32),
        jnp.zeros((BLOCK, HD), F32),
    )
    top, total, acc = lax.fori_loop(lo[tile], hi[tile], step, start)
    out_ref[0] = (acc / total).astype(BF16)


def attend(q, k, v, lo, hi, place, S, L):
    G = S // L
    rows = q.shape[1]
    return pl.pallas_call(
        functools.partial(attend_kernel, G, rows),
        out_shape=jax.ShapeDtypeStruct((L, rows, HD), BF16),
        grid_spec=pltpu.PrefetchScalarGridSpec(
            num_scalar_prefetch=3,
            grid=(L, rows // BLOCK),
            in_specs=[
                pl.BlockSpec((1, BLOCK, HD), lambda a, b, lo, hi, p: (a * G + p[0], b, 0)),
                VMEM,
                VMEM,
            ],
            out_specs=pl.BlockSpec((1, BLOCK, HD), lambda a, b, lo, hi, p: (a, b, 0)),
        ),
        compiler_params=pltpu.CompilerParams(vmem_limit_bytes=LIMIT),
        name="attend",
    )(lo, hi, place, q, k.reshape(S * rows, HD), v.reshape(S * rows, HD))


def spread_kernel(L, G, H, a_ref, out, send, recv):
    s, h = lax.axis_index("seq"), lax.axis_index("hid")
    c, k = s // G, s % G
    peers = [
        ((c + dc) % L, (h + dh) % H) for dh in range(H) for dc in range(L) if dc or dh
    ]
    ids = [{"seq": o * G + k, "hid": z} for o, z in peers]
    greet(ids)
    mine = h * L + c
    sent = []
    for t, (o, z) in enumerate(peers):
        copy = remote(
            a_ref.at[o], out.at[:, head_cols(mine)], send.at[t], recv.at[mine], ids[t]
        )
        copy.start()
        sent.append(copy)
    out[:, head_cols(mine)] = a_ref[c]
    for t, (o, z) in enumerate(peers):
        source = z * L + o
        remote(
            a_ref.at[o], out.at[:, head_cols(source)], send.at[t], recv.at[source], ids[t]
        ).wait_recv()
    for copy in sent:
        copy.wait_send()


def spread(a, S, L, H):
    rows = a.shape[1]
    return pl.pallas_call(
        functools.partial(spread_kernel, L, S // L, H),
        out_shape=jax.ShapeDtypeStruct((rows, H * L * HD), BF16),
        in_specs=[VMEM],
        out_specs=VMEM,
        scratch_shapes=[
            pltpu.SemaphoreType.DMA((H * L,)),
            pltpu.SemaphoreType.DMA((H * L,)),
        ],
        compiler_params=params(1),
        name="spread_attended",
    )(a)


def merge_kernel(
    L, G, H, a_ref, w_ref, x_ref, ls_ref, gain_ref, bias_ref, out,
    res, stats, lanes, place, weights, wsem, ssend, srecv, send1, recv1, send2, recv2,
):
    s, h = lax.axis_index("seq"), lax.axis_index("hid")
    c, k = s // G, s % G
    planes = [(h + t) % H for t in range(1, H)]
    places = [(c + t) % L for t in range(1, L)]
    mates = [(k + t) % G for t in range(1, G)]
    piece = w_ref.shape[2]
    loads = []
    for z in range(H):
        for n in range(L * G):
            at = (z * L * G + n) * piece
            copy = pltpu.make_async_copy(
                w_ref.at[n, z], weights.at[at : at + piece], wsem.at[n, z]
            )
            copy.start()
            loads.append(copy)
    greet(
        [{"hid": z} for z in planes]
        + [{"seq": o * G + k} for o in places]
        + [{"seq": c * G + m} for m in mates]
    )
    for copy in loads:
        copy.wait()
    rows, width = x_ref.shape
    sub = BLOCK // 4
    full = width // HD
    for b in range(rows // BLOCK):
        span = slice(b * BLOCK, (b + 1) * BLOCK)
        branch = jnp.dot(a_ref[span, :], weights[...], preferred_element_type=F32)
        value = x_ref[span, :].astype(F32) + ls_ref[...] * branch
        res[span, :] = value
        one = jnp.sum(value, axis=1, keepdims=True)
        two = jnp.sum(value * value, axis=1, keepdims=True)
        for n, column in ((0, one), (1, two)):
            summed = sum(column[q * sub : (q + 1) * sub] for q in range(4))
            stats[h, n, b * sub : (b + 1) * sub, :] = jnp.broadcast_to(summed, (sub, HD))
    sent = []
    for t, z in enumerate(planes):
        copy = remote(stats.at[h], stats.at[h], ssend.at[t], srecv.at[h], {"hid": z})
        copy.start()
        sent.append(copy)
    lanes[...] = jnp.zeros_like(lanes)
    row = lax.broadcasted_iota(jnp.int32, (4 * HD, 4 * HD), 0)
    col = lax.broadcasted_iota(jnp.int32, (4 * HD, 4 * HD), 1)
    place[...] = jnp.where(col == 4 * (row % HD) + lax.div(row, HD), 1.0, 0.0).astype(BF16)
    for t, z in enumerate(planes):
        remote(stats.at[z], stats.at[z], ssend.at[t], srecv.at[z], {"hid": z}).wait_recv()
    total = stats[0]
    for z in range(1, H):
        total = total + stats[z]
    total = total * (1.0 / (4 * width * H))
    mean = total[0]
    scale = lax.rsqrt(total[1] - mean * mean + 1e-05)
    for b in range(rows // BLOCK):
        part = slice(b * sub, (b + 1) * sub)
        mean_b, scale_b = mean[part, :1], scale[part, :1]
        for q in range(4):
            start = b * BLOCK + q * sub
            value = (res[start : start + sub, :] - mean_b) * scale_b
            value = (value * gain_ref[q : q + 1, :] + bias_ref[q : q + 1, :]).astype(BF16)
            for j in range(full):
                lanes[part, (4 * j + q) * HD : (4 * j + q + 1) * HD] = value[:, j * HD : (j + 1) * HD]
            if width % HD:
                at = (4 * full + q) * HD
                lanes[part, at : at + width % HD] = value[:, full * HD :]
    for j in range(full):
        cols = slice(4 * j * HD, 4 * (j + 1) * HD)
        out[s, :, cols] = jnp.dot(
            lanes[:, cols], place[...], preferred_element_type=F32
        ).astype(BF16)
    if width % HD:
        cols = slice(4 * full * HD, 4 * (full + 1) * HD)
        left = 4 * (width % HD)
        last = jnp.dot(lanes[:, cols], place[...], preferred_element_type=F32)
        out[s, :, 4 * full * HD :] = last[:, :left].astype(BF16)
    for t, o in enumerate(places):
        copy = remote(out.at[s], out.at[s], send1.at[t], recv1.at[c], {"seq": o * G + k})
        copy.start()
        sent.append(copy)

    def share(t, slot, home):
        for u, m in enumerate(mates):
            copy = remote(
                out.at[slot], out.at[slot], send2.at[t, u], recv2.at[home, k], {"seq": c * G + m}
            )
            copy.start()
            sent.append(copy)

    share(0, s, c)
    for t in range(1, L):
        o = (c - t + L) % L
        slot = o * G + k
        remote(out.at[slot], out.at[slot], send1.at[0], recv1.at[o], {"seq": slot}).wait_recv()
        share(t, slot, o)
    for m in mates:
        for t in range(L):
            o = (c + t) % L
            slot = o * G + m
            remote(
                out.at[slot], out.at[slot], send2.at[0, 0], recv2.at[o, m], {"seq": c * G + m}
            ).wait_recv()
    for copy in sent:
        copy.wait_send()


def merge(a, w, x, ls, gain, bias, S, L, H):
    G = S // L
    rows, width = x.shape
    return pl.pallas_call(
        functools.partial(merge_kernel, L, G, H),
        out_shape=jax.ShapeDtypeStruct((S, rows // 4, 4 * width), BF16),
        in_specs=[VMEM, pl.BlockSpec(memory_space=pl.ANY)] + [VMEM] * 4,
        out_specs=VMEM,
        scratch_shapes=[
            pltpu.VMEM((rows, width), F32),
            pltpu.VMEM((H, 2, rows // 4, HD), F32),
            pltpu.VMEM((rows // 4, 4 * HD * pl.cdiv(width, HD)), BF16),
            pltpu.VMEM((4 * HD, 4 * HD), BF16),
            pltpu.VMEM((a.shape[1], width), BF16),
            pltpu.SemaphoreType.DMA((S, H)),
            pltpu.SemaphoreType.DMA((H,)),
            pltpu.SemaphoreType.DMA((H,)),
            pltpu.SemaphoreType.DMA((L,)),
            pltpu.SemaphoreType.DMA((L,)),
            pltpu.SemaphoreType.DMA((L, G)),
            pltpu.SemaphoreType.DMA((L, G)),
        ],
        compiler_params=params(2),
        name="merge_rows",
    )(a, w, x, ls, gain, bias)


def finish_kernel(
    g, H, m_ref, w_ref, slot_ref, bias_ref, text_ref, mask_ref, gain_ref, stream, normed,
    p_ref, parts, rows_out, rows_in, squares, send1, recv1, send2, recv2, send3, recv3,
):
    s, h = lax.axis_index("seq"), lax.axis_index("hid")
    c, k = s // g, s % g
    planes = [(h + t) % H for t in range(1, H)]
    off = c != h
    barrier = pltpu.get_barrier_semaphore()
    for z in planes:
        pl.semaphore_signal(barrier, inc=1, device_id={"hid": z}, device_id_type=MESH)
    for t in range(g):
        j = (k + t) % g
        partner = {"seq": g * h + j, "hid": c}
        if t:
            pl.semaphore_signal(barrier, inc=1, device_id=partner, device_id_type=MESH)
        else:
            @pl.when(off)
            def _():
                pl.semaphore_signal(barrier, inc=1, device_id=partner, device_id_type=MESH)
    pl.semaphore_wait(barrier, len(planes) + g - 1 + off.astype(jnp.int32))

    sent = []
    part_rows = stream.shape[0]
    width = bias_ref.shape[1]
    step_rows = 2 * part_rows if g % 2 == 0 else part_rows
    steps = g * part_rows // step_rows

    def project(t, carry):
        z = (h + 1 + t) % H
        for n in range(steps):
            base = z * (g * part_rows) + n * step_rows
            position = base + lax.broadcasted_iota(jnp.int32, (step_rows, 1), 0)
            chosen = jnp.where(position == slot_ref[...], 1.0, 0.0).astype(BF16)
            rows = jnp.dot(chosen, m_ref[...], preferred_element_type=F32).astype(BF16)
            p_ref[z, n * step_rows : (n + 1) * step_rows, :] = jnp.dot(
                rows, w_ref[...], preferred_element_type=F32
            ).astype(BF16)

        @pl.when(t < H - 1)
        def _():
            remote(p_ref.at[z], parts.at[h], send1.at[t], recv1.at[h], {"hid": z}).start()

        return carry

    lax.fori_loop(0, H, project, 0)
    for t, z in enumerate(planes):
        copy = remote(p_ref.at[z], parts.at[z], send1.at[t], recv1.at[z], {"hid": z})
        copy.wait_recv()
        sent.append(copy)
    for j in range(g):
        span = slice(j * part_rows, (j + 1) * part_rows)
        value = p_ref[h, span, :].astype(F32)
        for z in planes:
            value = value + parts[z, span, :].astype(F32)
        value = value + bias_ref[...]
        value = value * (lax.erf(value * F32(0.7071067811865476)) + 1.0) * 0.5
        rows_out[j] = jnp.where(
            mask_ref[span, :1] > 0.5, value, text_ref[span, :].astype(F32)
        ).astype(BF16)
    for t in range(g):
        j = (k + t) % g
        partner = {"seq": g * h + j, "hid": c}
        copy = remote(rows_out.at[j], rows_in.at[k], send2.at[t], recv2.at[k], partner)
        if t:
            copy.start()
            sent.append(copy)
        else:
            pl.when(off)(copy.start)

            @pl.when(jnp.logical_not(off))
            def _():
                rows_in[k] = rows_out[k]

    for t in range(g):
        j = (k + t) % g
        partner = {"seq": g * h + j, "hid": c}
        copy = remote(rows_out.at[j], rows_in.at[j], send2.at[t], recv2.at[j], partner)
        if t:
            copy.wait_recv()
        else:
            @pl.when(off)
            def _():
                copy.wait_recv()
                copy.wait_send()
    square = jnp.zeros((part_rows, 1), F32)
    for j in range(g):
        value = rows_in[j]
        stream[:, j * width : (j + 1) * width] = value
        value = value.astype(F32)
        square = square + jnp.sum(value * value, axis=1, keepdims=True)
    squares[h] = jnp.broadcast_to(square, squares.shape[1:])
    for t, z in enumerate(planes):
        copy = remote(squares.at[h], squares.at[h], send3.at[t], recv3.at[h], {"hid": z})
        copy.start()
        sent.append(copy)
    for t, z in enumerate(planes):
        remote(squares.at[z], squares.at[z], send3.at[t], recv3.at[z], {"hid": z}).wait_recv()
    total = squares[0]
    for z in range(1, H):
        total = total + squares[z]
    scale = lax.rsqrt(total * (1.0 / (g * width * H)) + 1e-05)[:, :1]
    normed[...] = (stream[...].astype(F32) * scale * gain_ref[...]).astype(BF16)
    for copy in sent:
        copy.wait_send()


def finish(merged, weight, slots, bias, text, mask, gain, S, H):
    g = S // H
    width = weight.shape[1]
    part_rows = text.shape[0] // g
    shape = jax.ShapeDtypeStruct((part_rows, g * width), BF16)
    return pl.pallas_call(
        functools.partial(finish_kernel, g, H),
        out_shape=(shape, shape),
        in_specs=[VMEM] * 7,
        out_specs=(VMEM, VMEM),
        scratch_shapes=[
            pltpu.VMEM((H, g * part_rows, width), BF16),
            pltpu.VMEM((H, g * part_rows, width), BF16),
            pltpu.VMEM((g, part_rows, width), BF16),
            pltpu.VMEM((g, part_rows, width), BF16),
            pltpu.VMEM((H, part_rows, HD), F32),
            pltpu.SemaphoreType.DMA((H,)),
            pltpu.SemaphoreType.DMA((H,)),
            pltpu.SemaphoreType.DMA((g,)),
            pltpu.SemaphoreType.DMA((g,)),
            pltpu.SemaphoreType.DMA((H,)),
            pltpu.SemaphoreType.DMA((H,)),
        ],
        compiler_params=params(3),
        name="finish_rows",
    )(merged, weight, slots, bias, text, mask, gain)


def grouping():
    new = jnp.arange(BLOCK, dtype=jnp.int32)
    half = SIDE // 2
    quarter = BLOCK // 4
    spot, rest = new // quarter, new % quarter
    pair, c2 = rest // half, rest % half
    old = (2 * pair + spot // 2) * SIDE + 2 * c2 + spot % 2
    return (old[:, None] == new[None, :]).astype(BF16)


def per_device(
    patches,
    norm_gain,
    query_weight,
    key_weight,
    value_weight,
    out_weight,
    layer_scale,
    merge_gain,
    merge_bias,
    proj_weight,
    proj_bias,
    text_rows,
    stream_gain,
    tile_counts,
    image_slots,
    text_slots,
):
    S, H = lax.axis_size("seq"), lax.axis_size("hid")
    s, h = lax.axis_index("seq"), lax.axis_index("hid")
    rows, depth = patches.shape
    L = query_weight.shape[1] // HD
    G = S // L
    quarter = depth // H

    head_rows = out_weight.shape[0]
    piece = head_rows // S
    own_rows = lax.dynamic_slice_in_dim(out_weight, s * piece, piece, 0)
    own_rows = own_rows.reshape(piece, H, quarter).transpose(1, 0, 2)

    grouped = jnp.einsum(
        "ij,bjd->bid", grouping(), patches.reshape(rows // BLOCK, BLOCK, depth),
        preferred_element_type=F32,
    ).astype(BF16).reshape(rows, depth)
    tokens_f = grouped.astype(F32)
    normed_in = (
        tokens_f * lax.rsqrt(jnp.mean(tokens_f * tokens_f, -1, keepdims=True) + 1e-06) * norm_gain
    ).astype(BF16)
    queries = (
        jnp.dot(normed_in, query_weight, preferred_element_type=F32) * HD ** (-0.5)
    ).astype(BF16)
    key_rows = jnp.dot(normed_in, key_weight, preferred_element_type=F32).astype(BF16)
    value_rows = jnp.dot(normed_in, value_weight, preferred_element_type=F32).astype(BF16)

    q_all, k_all, v_all, own_cols = exchange(
        queries, key_rows, value_rows, own_rows, S, L, H
    )
    out_cols = lax.all_gather(own_cols, "seq", axis=0, tiled=False)
    tiles = S * rows // TILE
    ends = jnp.cumsum(tile_counts).astype(jnp.int32)
    tile = jnp.arange(tiles, dtype=jnp.int32)
    after = tile[:, None] >= ends[None, :]
    lo = jnp.max(jnp.where(after, ends[None, :], 0), axis=1).astype(jnp.int32)
    hi = jnp.min(jnp.where(after, tiles, ends[None, :]), axis=1).astype(jnp.int32)
    place = (s % G).astype(jnp.int32).reshape(1)
    heads = attend(q_all, k_all, v_all, lo, hi, place, S, L)
    attended = spread(heads, S, L, H)

    own_tokens = lax.dynamic_slice_in_dim(grouped, h * quarter, quarter, 1)
    own_scale = lax.dynamic_slice_in_dim(layer_scale, h * quarter, quarter, 0)
    merged_normed = merge(
        attended,
        out_cols,
        own_tokens,
        own_scale.reshape(1, quarter),
        merge_gain.reshape(quarter, 4).T,
        merge_bias.reshape(quarter, 4).T,
        S,
        L,
        H,
    )
    stream_size = image_slots.shape[0] + text_slots.shape[0]
    share = stream_size // H
    width = proj_weight.shape[1]
    own_positions = h * share + jnp.arange(share, dtype=jnp.int32)
    is_text = own_positions[:, None] == text_slots[None, :]
    text = jnp.dot(is_text.astype(BF16), text_rows, preferred_element_type=F32).astype(BF16)
    is_image = jnp.where(jnp.any(is_text, axis=1, keepdims=True), 0.0, 1.0)
    mask = jnp.broadcast_to(is_image.astype(F32), (share, HD))
    return finish(
        merged_normed.reshape(S * rows // 4, 4 * quarter),
        proj_weight,
        image_slots.reshape(1, image_slots.shape[0]),
        proj_bias.reshape(1, width),
        text,
        mask,
        stream_gain.reshape(1, stream_gain.shape[0]),
        S,
        H,
    )


def solution(mesh):
    return jax.shard_map(
        per_device,
        mesh=mesh,
        in_specs=(
            P("seq", None),
            P(),
            P(None, "hid"),
            P(None, "hid"),
            P(None, "hid"),
            P("hid", None),
            P(),
            P("hid"),
            P("hid"),
            P("hid", "seq"),
            P("seq"),
            P(None, "seq"),
            P("hid"),
            P(),
            P(),
            P(),
        ),
        out_specs=(P("seq", "hid"), P("seq", "hid")),
        check_vma=False,
    )
```

```python
import functools

import jax
import jax.numpy as jnp
from jax import lax
from jax.experimental import pallas as pl
from jax.experimental.pallas import tpu as pltpu
from jax.sharding import PartitionSpec as P

HD = 128
SIDE = 32
TILE = SIDE * SIDE
BLOCK = 128
MESH = pl.DeviceIdType.MESH
F32 = jnp.float32
BF16 = jnp.bfloat16
VMEM = pl.BlockSpec(memory_space=pltpu.VMEM)
LIMIT = 50 * 1024 * 1024


def params(number):
    return pltpu.CompilerParams(
        collective_id=number, has_side_effects=True, vmem_limit_bytes=LIMIT
    )


def greet(peers):
    barrier = pltpu.get_barrier_semaphore()
    for peer in peers:
        pl.semaphore_signal(barrier, inc=1, device_id=peer, device_id_type=MESH)
    pl.semaphore_wait(barrier, len(peers))


def remote(src, dst, send_sem, recv_sem, peer):
    return pltpu.make_async_remote_copy(
        src_ref=src,
        dst_ref=dst,
        send_sem=send_sem,
        recv_sem=recv_sem,
        device_id=peer,
        device_id_type=MESH,
    )


def head_cols(index):
    return pl.ds(pl.multiple_of(index * HD, HD), HD)


def exchange_kernel(
    L, G, H, q_ref, k_ref, v_ref, w_ref, qo, ko, vo, wo, send1, recv1, send2, recv2, send3, recv3
):
    s, h = lax.axis_index("seq"), lax.axis_index("hid")
    c, k = s // G, s % G
    planes = [(h + t) % H for t in range(1, H)]
    places = [(c + t) % L for t in range(1, L)]
    mates = [(k + t) % G for t in range(1, G)]
    greet(
        [{"hid": z} for z in planes]
        + [{"seq": o * G + k} for o in places]
        + [{"seq": c * G + m} for m in mates]
    )
    ins, outs = (k_ref, v_ref, q_ref), (ko, vo, qo)
    sent = []
    for t, o in enumerate(places):
        for a in range(3):
            copy = remote(
                ins[a].at[:, head_cols(o)], outs[a].at[s], send1.at[t, a], recv1.at[c, a],
                {"seq": o * G + k},
            )
            copy.start()
            sent.append(copy)
    for t, z in enumerate(planes):
        copy = remote(w_ref.at[z], wo.at[h], send3.at[t], recv3.at[h], {"hid": z})
        copy.start()
        sent.append(copy)
    wo[h] = w_ref[h]
    own = head_cols(c)
    for a in range(3):
        outs[a][s] = ins[a][:, own]

    def share(t, slot, home):
        for u, m in enumerate(mates):
            for a in range(2):
                copy = remote(
                    outs[a].at[slot], outs[a].at[slot], send2.at[t, u, a], recv2.at[home, k, a],
                    {"seq": c * G + m},
                )
                copy.start()
                sent.append(copy)

    share(0, s, c)
    for t in range(1, L):
        o = (c - t + L) % L
        for a in range(3):
            remote(
                outs[a].at[o * G + k], outs[a].at[o * G + k], send1.at[0, a], recv1.at[o, a],
                {"seq": o * G + k},
            ).wait_recv()
        share(t, o * G + k, o)
    for m in mates:
        for t in range(L):
            o = (c + t) % L
            for a in range(2):
                remote(
                    outs[a].at[o * G + m], outs[a].at[o * G + m], send2.at[0, 0, a],
                    recv2.at[o, m, a], {"seq": c * G + m},
                ).wait_recv()
    for t, z in enumerate(planes):
        remote(w_ref.at[z], wo.at[z], send3.at[t], recv3.at[z], {"hid": z}).wait_recv()
    for copy in sent:
        copy.wait_send()


def exchange(q, k, v, w, S, L, H):
    G = S // L
    rows = q.shape[0]
    shape = jax.ShapeDtypeStruct((S, rows, HD), BF16)
    return pl.pallas_call(
        functools.partial(exchange_kernel, L, G, H),
        out_shape=(shape,) * 3 + (jax.ShapeDtypeStruct(w.shape, w.dtype),),
        in_specs=[VMEM] * 4,
        out_specs=(VMEM,) * 4,
        scratch_shapes=[
            pltpu.SemaphoreType.DMA((L, 3)),
            pltpu.SemaphoreType.DMA((L, 3)),
            pltpu.SemaphoreType.DMA((L, G, 2)),
            pltpu.SemaphoreType.DMA((L, G, 2)),
            pltpu.SemaphoreType.DMA((H,)),
            pltpu.SemaphoreType.DMA((H,)),
        ],
        compiler_params=params(0),
        name="exchange_heads",
    )(q, k, v, w)


def attend_kernel(
    L, G, H, tiles, q_ref, k_ref, v_ref, bias_ref, out, heads, send, recv
):
    s, h = lax.axis_index("seq"), lax.axis_index("hid")
    c, k = s // G, s % G
    rows = heads.shape[1]
    peers = [
        ((c + dc) % L, (h + dh) % H)
        for dc in (*range(1, L), 0)
        for dh in (*range(1, H), 0)
        if dc or dh
    ]
    ids = [{"seq": o * G + k, "hid": z} for o, z in peers]
    greet(ids)
    mine = h * L + c
    sent = []
    for n in range(L):
        o = (c + n + 1) % L
        slot = o * G + k

        def block(i, carry):
            at = pl.multiple_of(i * BLOCK, BLOCK)
            tile = (slot * rows + i * BLOCK) // TILE
            q = q_ref[slot, pl.ds(at, BLOCK), :]

            def step(t, state):
                top, total, acc = state
                span = pl.ds(pl.multiple_of(t * TILE, TILE), TILE)
                scores = lax.dot_general(
                    q, k_ref[span, :], (((1,), (1,)), ((), ())), preferred_element_type=F32
                )
                scores = scores + bias_ref[tile * tiles + t][:, :1]
                new_top = jnp.maximum(top, jnp.max(scores, axis=1, keepdims=True))
                factor = jnp.exp(top - new_top)
                weights = jnp.exp(scores - new_top)
                total = total * factor + jnp.sum(weights, axis=1, keepdims=True)
                acc = acc * factor + jnp.dot(
                    weights.astype(BF16), v_ref[span, :], preferred_element_type=F32
                )
                return new_top, total, acc

            state = (
                jnp.full((BLOCK, 1), -1e30, F32),
                jnp.zeros((BLOCK, 1), F32),
                jnp.zeros((BLOCK, HD), F32),
            )
            if tiles <= 4:
                for t in range(tiles):
                    state = step(t, state)
            else:
                state = lax.fori_loop(0, tiles, step, state)
            heads[o, pl.ds(at, BLOCK), :] = (state[2] / state[1]).astype(BF16)
            return carry

        lax.fori_loop(0, rows // BLOCK, block, 0)
        for t in range(n * H, min((n + 1) * H, len(peers))):
            copy = remote(
                heads.at[o], out.at[:, head_cols(mine)], send.at[t], recv.at[mine], ids[t]
            )
            copy.start()
            sent.append(copy)
    out[:, head_cols(mine)] = heads[c]
    for t, (o, z) in enumerate(peers):
        source = z * L + o
        remote(
            heads.at[o], out.at[:, head_cols(source)], send.at[t], recv.at[source], ids[t]
        ).wait_recv()
    for copy in sent:
        copy.wait_send()


def attend(q, k, v, bias, S, L, H):
    rows = q.shape[1]
    return pl.pallas_call(
        functools.partial(attend_kernel, L, S // L, H, S * rows // TILE),
        out_shape=jax.ShapeDtypeStruct((rows, H * L * HD), BF16),
        in_specs=[VMEM] * 4,
        out_specs=VMEM,
        scratch_shapes=[
            pltpu.VMEM((L, rows, HD), BF16),
            pltpu.SemaphoreType.DMA((H * L,)),
            pltpu.SemaphoreType.DMA((H * L,)),
        ],
        compiler_params=params(1),
        name="attend_and_spread",
    )(q, k.reshape(S * rows, HD), v.reshape(S * rows, HD), bias)


def merge_kernel(
    L, G, H, a_ref, w_ref, x_ref, ls_ref, gain_ref, bias_ref, out,
    res, stats, lanes, place, weights, wsem, ssend, srecv, send1, recv1, send2, recv2,
):
    s, h = lax.axis_index("seq"), lax.axis_index("hid")
    c, k = s // G, s % G
    planes = [(h + t) % H for t in range(1, H)]
    places = [(c + t) % L for t in range(1, L)]
    mates = [(k + t) % G for t in range(1, G)]
    piece = w_ref.shape[2]
    loads = []
    for z in range(H):
        for n in range(L * G):
            at = (z * L * G + n) * piece
            copy = pltpu.make_async_copy(
                w_ref.at[n, z], weights.at[at : at + piece], wsem.at[n, z]
            )
            copy.start()
            loads.append(copy)
    greet(
        [{"hid": z} for z in planes]
        + [{"seq": o * G + k} for o in places]
        + [{"seq": c * G + m} for m in mates]
    )
    for copy in loads:
        copy.wait()
    rows, width = x_ref.shape
    sub = BLOCK // 4
    full = width // HD
    for b in range(rows // BLOCK):
        span = slice(b * BLOCK, (b + 1) * BLOCK)
        branch = jnp.dot(a_ref[span, :], weights[...], preferred_element_type=F32)
        value = x_ref[span, :].astype(F32) + ls_ref[...] * branch
        res[span, :] = value
        one = jnp.sum(value, axis=1, keepdims=True)
        two = jnp.sum(value * value, axis=1, keepdims=True)
        for n, column in ((0, one), (1, two)):
            summed = sum(column[q * sub : (q + 1) * sub] for q in range(4))
            stats[h, n, b * sub : (b + 1) * sub, :] = jnp.broadcast_to(summed, (sub, HD))
    sent = []
    for t, z in enumerate(planes):
        copy = remote(stats.at[h], stats.at[h], ssend.at[t], srecv.at[h], {"hid": z})
        copy.start()
        sent.append(copy)
    lanes[...] = jnp.zeros_like(lanes)
    row = lax.broadcasted_iota(jnp.int32, (4 * HD, 4 * HD), 0)
    col = lax.broadcasted_iota(jnp.int32, (4 * HD, 4 * HD), 1)
    place[...] = jnp.where(col == 4 * (row % HD) + lax.div(row, HD), 1.0, 0.0).astype(BF16)
    for t, z in enumerate(planes):
        remote(stats.at[z], stats.at[z], ssend.at[t], srecv.at[z], {"hid": z}).wait_recv()
    total = stats[0]
    for z in range(1, H):
        total = total + stats[z]
    total = total * (1.0 / (4 * width * H))
    mean = total[0]
    scale = lax.rsqrt(total[1] - mean * mean + 1e-05)
    for b in range(rows // BLOCK):
        part = slice(b * sub, (b + 1) * sub)
        mean_b, scale_b = mean[part, :1], scale[part, :1]
        for q in range(4):
            start = b * BLOCK + q * sub
            value = (res[start : start + sub, :] - mean_b) * scale_b
            value = (value * gain_ref[q : q + 1, :] + bias_ref[q : q + 1, :]).astype(BF16)
            for j in range(full):
                lanes[part, (4 * j + q) * HD : (4 * j + q + 1) * HD] = value[:, j * HD : (j + 1) * HD]
            if width % HD:
                at = (4 * full + q) * HD
                lanes[part, at : at + width % HD] = value[:, full * HD :]
    for j in range(full):
        cols = slice(4 * j * HD, 4 * (j + 1) * HD)
        out[s, :, cols] = jnp.dot(
            lanes[:, cols], place[...], preferred_element_type=F32
        ).astype(BF16)
    if width % HD:
        cols = slice(4 * full * HD, 4 * (full + 1) * HD)
        left = 4 * (width % HD)
        last = jnp.dot(lanes[:, cols], place[...], preferred_element_type=F32)
        out[s, :, 4 * full * HD :] = last[:, :left].astype(BF16)
    for t, o in enumerate(places):
        copy = remote(out.at[s], out.at[s], send1.at[t], recv1.at[c], {"seq": o * G + k})
        copy.start()
        sent.append(copy)

    def share(t, slot, home):
        for u, m in enumerate(mates):
            copy = remote(
                out.at[slot], out.at[slot], send2.at[t, u], recv2.at[home, k], {"seq": c * G + m}
            )
            copy.start()
            sent.append(copy)

    share(0, s, c)
    for t in range(1, L):
        o = (c - t + L) % L
        slot = o * G + k
        remote(out.at[slot], out.at[slot], send1.at[0], recv1.at[o], {"seq": slot}).wait_recv()
        share(t, slot, o)
    for m in mates:
        for t in range(L):
            o = (c + t) % L
            slot = o * G + m
            remote(
                out.at[slot], out.at[slot], send2.at[0, 0], recv2.at[o, m], {"seq": c * G + m}
            ).wait_recv()
    for copy in sent:
        copy.wait_send()


def merge(a, w, x, ls, gain, bias, S, L, H):
    G = S // L
    rows, width = x.shape
    return pl.pallas_call(
        functools.partial(merge_kernel, L, G, H),
        out_shape=jax.ShapeDtypeStruct((S, rows // 4, 4 * width), BF16),
        in_specs=[VMEM, pl.BlockSpec(memory_space=pl.ANY)] + [VMEM] * 4,
        out_specs=VMEM,
        scratch_shapes=[
            pltpu.VMEM((rows, width), F32),
            pltpu.VMEM((H, 2, rows // 4, HD), F32),
            pltpu.VMEM((rows // 4, 4 * HD * pl.cdiv(width, HD)), BF16),
            pltpu.VMEM((4 * HD, 4 * HD), BF16),
            pltpu.VMEM((a.shape[1], width), BF16),
            pltpu.SemaphoreType.DMA((S, H)),
            pltpu.SemaphoreType.DMA((H,)),
            pltpu.SemaphoreType.DMA((H,)),
            pltpu.SemaphoreType.DMA((L,)),
            pltpu.SemaphoreType.DMA((L,)),
            pltpu.SemaphoreType.DMA((L, G)),
            pltpu.SemaphoreType.DMA((L, G)),
        ],
        compiler_params=params(2),
        name="merge_rows",
    )(a, w, x, ls, gain, bias)


def finish_kernel(
    g, H, m_ref, w_ref, slot_ref, bias_ref, text_ref, mask_ref, gain_ref, stream, normed,
    p_ref, parts, rows_out, rows_in, squares, send1, recv1, send2, recv2, send3, recv3,
):
    s, h = lax.axis_index("seq"), lax.axis_index("hid")
    c, k = s // g, s % g
    planes = [(h + t) % H for t in range(1, H)]
    off = c != h
    barrier = pltpu.get_barrier_semaphore()
    for z in planes:
        pl.semaphore_signal(barrier, inc=1, device_id={"hid": z}, device_id_type=MESH)
    for t in range(g):
        j = (k + t) % g
        partner = {"seq": g * h + j, "hid": c}
        if t:
            pl.semaphore_signal(barrier, inc=1, device_id=partner, device_id_type=MESH)
        else:
            @pl.when(off)
            def _():
                pl.semaphore_signal(barrier, inc=1, device_id=partner, device_id_type=MESH)
    pl.semaphore_wait(barrier, len(planes) + g - 1 + off.astype(jnp.int32))

    sent = []
    part_rows = stream.shape[0]
    width = bias_ref.shape[1]
    step_rows = 2 * part_rows if g % 2 == 0 else part_rows
    steps = g * part_rows // step_rows

    def part(j):
        return slice(j * part_rows, (j + 1) * part_rows)

    def first_send(t, z, j):
        return remote(
            p_ref.at[z, part(j)], parts.at[h, part(j)], send1.at[t, j], recv1.at[h, j], {"hid": z}
        )

    def project(t, carry):
        z = (h + 1 + t) % H

        def some(n, inner):
            at = n * step_rows
            base = z * (g * part_rows) + at
            position = base + lax.broadcasted_iota(jnp.int32, (step_rows, 1), 0)
            chosen = jnp.where(position == slot_ref[...], 1.0, 0.0).astype(BF16)
            rows = jnp.dot(chosen, m_ref[...], preferred_element_type=F32).astype(BF16)
            value = jnp.dot(rows, w_ref[...], preferred_element_type=F32).astype(BF16)
            if steps == 1:
                p_ref[z] = value
            else:
                p_ref[z, pl.ds(pl.multiple_of(at, step_rows), step_rows), :] = value
            return inner

        if steps == 1:
            some(0, 0)
        else:
            lax.fori_loop(0, steps, some, 0)

        @pl.when(t < H - 1)
        def _():
            first_send(t, z, 0).start()

        return carry

    lax.fori_loop(0, H, project, 0)
    for j in range(1, g):
        for t, z in enumerate(planes):
            first_send(t, z, j).start()
    for j in range(g):
        span = part(j)
        value = p_ref[h, span, :].astype(F32)
        for t, z in enumerate(planes):
            copy = remote(
                p_ref.at[z, span], parts.at[z, span], send1.at[t, j], recv1.at[z, j], {"hid": z}
            )
            copy.wait_recv()
            sent.append(copy)
            value = value + parts[z, span, :].astype(F32)
        value = value + bias_ref[...]
        value = value * (lax.erf(value * F32(0.7071067811865476)) + 1.0) * 0.5
        rows_out[j] = jnp.where(
            mask_ref[span, :1] > 0.5, value, text_ref[span, :].astype(F32)
        ).astype(BF16)
        away = jnp.logical_or(off, k != j)

        @pl.when(away)
        def _():
            remote(
                rows_out.at[j], rows_in.at[k], send2.at[j], recv2.at[k],
                {"seq": g * h + j, "hid": c},
            ).start()

        @pl.when(jnp.logical_not(away))
        def _():
            rows_in[k] = rows_out[j]

    for j in range(g):
        @pl.when(jnp.logical_or(off, k != j))
        def _():
            copy = remote(
                rows_out.at[j], rows_in.at[j], send2.at[j], recv2.at[j],
                {"seq": g * h + j, "hid": c},
            )
            copy.wait_recv()
            copy.wait_send()

    square = jnp.zeros((part_rows, 1), F32)
    for j in range(g):
        value = rows_in[j]
        stream[:, j * width : (j + 1) * width] = value
        value = value.astype(F32)
        square = square + jnp.sum(value * value, axis=1, keepdims=True)
    squares[h] = jnp.broadcast_to(square, squares.shape[1:])
    for t, z in enumerate(planes):
        copy = remote(squares.at[h], squares.at[h], send3.at[t], recv3.at[h], {"hid": z})
        copy.start()
        sent.append(copy)
    for t, z in enumerate(planes):
        remote(squares.at[z], squares.at[z], send3.at[t], recv3.at[z], {"hid": z}).wait_recv()
    total = squares[0]
    for z in range(1, H):
        total = total + squares[z]
    scale = lax.rsqrt(total * (1.0 / (g * width * H)) + 1e-05)[:, :1]
    normed[...] = (stream[...].astype(F32) * scale * gain_ref[...]).astype(BF16)
    for copy in sent:
        copy.wait_send()


def finish(merged, weight, slots, bias, text, mask, gain, S, H):
    g = S // H
    width = weight.shape[1]
    part_rows = text.shape[0] // g
    shape = jax.ShapeDtypeStruct((part_rows, g * width), BF16)
    return pl.pallas_call(
        functools.partial(finish_kernel, g, H),
        out_shape=(shape, shape),
        in_specs=[VMEM] * 7,
        out_specs=(VMEM, VMEM),
        scratch_shapes=[
            pltpu.VMEM((H, g * part_rows, width), BF16),
            pltpu.VMEM((H, g * part_rows, width), BF16),
            pltpu.VMEM((g, part_rows, width), BF16),
            pltpu.VMEM((g, part_rows, width), BF16),
            pltpu.VMEM((H, part_rows, HD), F32),
            pltpu.SemaphoreType.DMA((H, g)),
            pltpu.SemaphoreType.DMA((H, g)),
            pltpu.SemaphoreType.DMA((g,)),
            pltpu.SemaphoreType.DMA((g,)),
            pltpu.SemaphoreType.DMA((H,)),
            pltpu.SemaphoreType.DMA((H,)),
        ],
        compiler_params=params(3),
        name="finish_rows",
    )(merged, weight, slots, bias, text, mask, gain)


def grouping():
    new = jnp.arange(BLOCK, dtype=jnp.int32)
    half = SIDE // 2
    quarter = BLOCK // 4
    spot, rest = new // quarter, new % quarter
    pair, c2 = rest // half, rest % half
    old = (2 * pair + spot // 2) * SIDE + 2 * c2 + spot % 2
    return (old[:, None] == new[None, :]).astype(BF16)


def per_device(
    patches,
    norm_gain,
    query_weight,
    key_weight,
    value_weight,
    out_weight,
    layer_scale,
    merge_gain,
    merge_bias,
    proj_weight,
    proj_bias,
    text_rows,
    stream_gain,
    tile_counts,
    image_slots,
    text_slots,
):
    S, H = lax.axis_size("seq"), lax.axis_size("hid")
    s, h = lax.axis_index("seq"), lax.axis_index("hid")
    rows, depth = patches.shape
    L = query_weight.shape[1] // HD
    G = S // L
    quarter = depth // H

    head_rows = out_weight.shape[0]
    piece = head_rows // S
    own_rows = lax.dynamic_slice_in_dim(out_weight, s * piece, piece, 0)
    own_rows = own_rows.reshape(piece, H, quarter).transpose(1, 0, 2)

    grouped = jnp.einsum(
        "ij,bjd->bid", grouping(), patches.reshape(rows // BLOCK, BLOCK, depth),
        preferred_element_type=F32,
    ).astype(BF16).reshape(rows, depth)
    tokens_f = grouped.astype(F32)
    normed_in = (
        tokens_f * lax.rsqrt(jnp.mean(tokens_f * tokens_f, -1, keepdims=True) + 1e-06) * norm_gain
    ).astype(BF16)
    queries = (
        jnp.dot(normed_in, query_weight, preferred_element_type=F32) * HD ** (-0.5)
    ).astype(BF16)
    key_rows = jnp.dot(normed_in, key_weight, preferred_element_type=F32).astype(BF16)
    value_rows = jnp.dot(normed_in, value_weight, preferred_element_type=F32).astype(BF16)

    q_all, k_all, v_all, own_cols = exchange(
        queries, key_rows, value_rows, own_rows, S, L, H
    )
    out_cols = lax.all_gather(own_cols, "seq", axis=0, tiled=False)
    tiles = S * rows // TILE
    ends = jnp.cumsum(tile_counts).astype(jnp.int32)
    tile = jnp.arange(tiles, dtype=jnp.int32)
    image = jnp.sum((tile[:, None] >= ends[None, :]).astype(jnp.int32), axis=1)
    bias = jnp.where(image[:, None] == image[None, :], 0.0, -1e30).astype(F32)
    bias = jnp.broadcast_to(bias.reshape(tiles * tiles, 1, 1), (tiles * tiles, 1, HD))
    attended = attend(q_all, k_all, v_all, bias, S, L, H)

    own_tokens = lax.dynamic_slice_in_dim(grouped, h * quarter, quarter, 1)
    own_scale = lax.dynamic_slice_in_dim(layer_scale, h * quarter, quarter, 0)
    merged_normed = merge(
        attended,
        out_cols,
        own_tokens,
        own_scale.reshape(1, quarter),
        merge_gain.reshape(quarter, 4).T,
        merge_bias.reshape(quarter, 4).T,
        S,
        L,
        H,
    )
    stream_size = image_slots.shape[0] + text_slots.shape[0]
    share = stream_size // H
    width = proj_weight.shape[1]
    own_positions = h * share + jnp.arange(share, dtype=jnp.int32)
    is_text = own_positions[:, None] == text_slots[None, :]
    text = jnp.dot(is_text.astype(BF16), text_rows, preferred_element_type=F32).astype(BF16)
    is_image = jnp.where(jnp.any(is_text, axis=1, keepdims=True), 0.0, 1.0)
    mask = jnp.broadcast_to(is_image.astype(F32), (share, HD))
    return finish(
        merged_normed.reshape(S * rows // 4, 4 * quarter),
        proj_weight,
        image_slots.reshape(1, image_slots.shape[0]),
        proj_bias.reshape(1, width),
        text,
        mask,
        stream_gain.reshape(1, stream_gain.shape[0]),
        S,
        H,
    )


def solution(mesh):
    return jax.shard_map(
        per_device,
        mesh=mesh,
        in_specs=(
            P("seq", None),
            P(),
            P(None, "hid"),
            P(None, "hid"),
            P(None, "hid"),
            P("hid", None),
            P(),
            P("hid"),
            P("hid"),
            P("hid", "seq"),
            P("seq"),
            P(None, "seq"),
            P("hid"),
            P(),
            P(),
            P(),
        ),
        out_specs=(P("seq", "hid"), P("seq", "hid")),
        check_vma=False,
    )
```

```python
import functools

import jax
import jax.numpy as jnp
from jax import lax
from jax.experimental import pallas as pl
from jax.experimental.pallas import tpu as pltpu
from jax.sharding import PartitionSpec as P

HD = 128
SIDE = 32
TILE = SIDE * SIDE
BLOCK = 128
MESH = pl.DeviceIdType.MESH
F32 = jnp.float32
BF16 = jnp.bfloat16
VMEM = pl.BlockSpec(memory_space=pltpu.VMEM)
LIMIT = 50 * 1024 * 1024


def params(number):
    return pltpu.CompilerParams(
        collective_id=number, has_side_effects=True, vmem_limit_bytes=LIMIT
    )


def greet(peers):
    barrier = pltpu.get_barrier_semaphore()
    for peer in peers:
        pl.semaphore_signal(barrier, inc=1, device_id=peer, device_id_type=MESH)
    pl.semaphore_wait(barrier, len(peers))


def remote(src, dst, send_sem, recv_sem, peer):
    return pltpu.make_async_remote_copy(
        src_ref=src,
        dst_ref=dst,
        send_sem=send_sem,
        recv_sem=recv_sem,
        device_id=peer,
        device_id_type=MESH,
    )


def head_cols(index):
    return pl.ds(pl.multiple_of(index * HD, HD), HD)


def exchange_kernel(
    L, G, H, q_ref, k_ref, v_ref, w_ref, qo, ko, vo, wo, send1, recv1, send2, recv2, send3, recv3
):
    s, h = lax.axis_index("seq"), lax.axis_index("hid")
    c, k = s // G, s % G
    planes = [(h + t) % H for t in range(1, H)]
    places = [(c + t) % L for t in range(1, L)]
    mates = [(k + t) % G for t in range(1, G)]
    greet(
        [{"hid": z} for z in planes]
        + [{"seq": o * G + k} for o in places]
        + [{"seq": c * G + m} for m in mates]
    )
    ins, outs = (k_ref, v_ref, q_ref), (ko, vo, qo)
    sent = []
    for t, o in enumerate(places):
        for a in range(3):
            copy = remote(
                ins[a].at[:, head_cols(o)], outs[a].at[s], send1.at[t, a], recv1.at[c, a],
                {"seq": o * G + k},
            )
            copy.start()
            sent.append(copy)
    for t, z in enumerate(planes):
        copy = remote(w_ref.at[z], wo.at[h], send3.at[t], recv3.at[h], {"hid": z})
        copy.start()
        sent.append(copy)
    wo[h] = w_ref[h]
    own = head_cols(c)
    for a in range(3):
        outs[a][s] = ins[a][:, own]

    def share(t, slot, home):
        for u, m in enumerate(mates):
            for a in range(2):
                copy = remote(
                    outs[a].at[slot], outs[a].at[slot], send2.at[t, u, a], recv2.at[home, k, a],
                    {"seq": c * G + m},
                )
                copy.start()
                sent.append(copy)

    share(0, s, c)
    for t in range(1, L):
        o = (c - t + L) % L
        for a in range(3):
            remote(
                outs[a].at[o * G + k], outs[a].at[o * G + k], send1.at[0, a], recv1.at[o, a],
                {"seq": o * G + k},
            ).wait_recv()
        share(t, o * G + k, o)
    for m in mates:
        for t in range(L):
            o = (c + t) % L
            for a in range(2):
                remote(
                    outs[a].at[o * G + m], outs[a].at[o * G + m], send2.at[0, 0, a],
                    recv2.at[o, m, a], {"seq": c * G + m},
                ).wait_recv()
    for t, z in enumerate(planes):
        remote(w_ref.at[z], wo.at[z], send3.at[t], recv3.at[z], {"hid": z}).wait_recv()
    for copy in sent:
        copy.wait_send()


def exchange(q, k, v, w, S, L, H):
    G = S // L
    rows = q.shape[0]
    shape = jax.ShapeDtypeStruct((S, rows, HD), BF16)
    return pl.pallas_call(
        functools.partial(exchange_kernel, L, G, H),
        out_shape=(shape,) * 3 + (jax.ShapeDtypeStruct(w.shape, w.dtype),),
        in_specs=[VMEM] * 4,
        out_specs=(VMEM,) * 4,
        scratch_shapes=[
            pltpu.SemaphoreType.DMA((L, 3)),
            pltpu.SemaphoreType.DMA((L, 3)),
            pltpu.SemaphoreType.DMA((L, G, 2)),
            pltpu.SemaphoreType.DMA((L, G, 2)),
            pltpu.SemaphoreType.DMA((H,)),
            pltpu.SemaphoreType.DMA((H,)),
        ],
        compiler_params=params(0),
        name="exchange_heads",
    )(q, k, v, w)


def attend_kernel(
    L, G, H, tiles, q_ref, k_ref, v_ref, bias_ref, out, heads, send, recv
):
    s, h = lax.axis_index("seq"), lax.axis_index("hid")
    c, k = s // G, s % G
    rows = heads.shape[1]
    peers = [
        ((c + dc) % L, (h + dh) % H)
        for dc in (*range(1, L), 0)
        for dh in (*range(1, H), 0)
        if dc or dh
    ]
    ids = [{"seq": o * G + k, "hid": z} for o, z in peers]
    greet(ids)
    mine = h * L + c
    sent = []
    for n in range(L):
        o = (c + n + 1) % L
        slot = o * G + k

        def block(i, carry):
            at = pl.multiple_of(i * BLOCK, BLOCK)
            tile = (slot * rows + i * BLOCK) // TILE
            q = q_ref[slot, pl.ds(at, BLOCK), :]

            def step(t, state):
                top, total, acc = state
                span = pl.ds(pl.multiple_of(t * TILE, TILE), TILE)
                scores = lax.dot_general(
                    q, k_ref[span, :], (((1,), (1,)), ((), ())), preferred_element_type=F32
                )
                scores = scores + bias_ref[tile * tiles + t][:, :1]
                new_top = jnp.maximum(top, jnp.max(scores, axis=1, keepdims=True))
                factor = jnp.exp(top - new_top)
                weights = jnp.exp(scores - new_top)
                total = total * factor + jnp.sum(weights, axis=1, keepdims=True)
                acc = acc * factor + jnp.dot(
                    weights.astype(BF16), v_ref[span, :], preferred_element_type=F32
                )
                return new_top, total, acc

            state = (
                jnp.full((BLOCK, 1), -1e30, F32),
                jnp.zeros((BLOCK, 1), F32),
                jnp.zeros((BLOCK, HD), F32),
            )
            if tiles <= 4:
                for t in range(tiles):
                    state = step(t, state)
            else:
                state = lax.fori_loop(0, tiles, step, state)
            heads[o, pl.ds(at, BLOCK), :] = (state[2] / state[1]).astype(BF16)
            return carry

        lax.fori_loop(0, rows // BLOCK, block, 0)
        for t in range(n * H, min((n + 1) * H, len(peers))):
            copy = remote(
                heads.at[o], out.at[:, head_cols(mine)], send.at[t], recv.at[mine], ids[t]
            )
            copy.start()
            sent.append(copy)
    out[:, head_cols(mine)] = heads[c]
    for t, (o, z) in enumerate(peers):
        source = z * L + o
        remote(
            heads.at[o], out.at[:, head_cols(source)], send.at[t], recv.at[source], ids[t]
        ).wait_recv()
    for copy in sent:
        copy.wait_send()


def attend(q, k, v, bias, S, L, H):
    rows = q.shape[1]
    return pl.pallas_call(
        functools.partial(attend_kernel, L, S // L, H, S * rows // TILE),
        out_shape=jax.ShapeDtypeStruct((rows, H * L * HD), BF16),
        in_specs=[VMEM] * 4,
        out_specs=VMEM,
        scratch_shapes=[
            pltpu.VMEM((L, rows, HD), BF16),
            pltpu.SemaphoreType.DMA((H * L,)),
            pltpu.SemaphoreType.DMA((H * L,)),
        ],
        compiler_params=params(1),
        name="attend_and_spread",
    )(q, k.reshape(S * rows, HD), v.reshape(S * rows, HD), bias)


def merge_kernel(
    L, G, H, a_ref, w_ref, x_ref, ls_ref, affine_ref, out,
    res, stats, lanes, affine, place, weights, wsem, ssend, srecv, send1, recv1, send2, recv2,
):
    s, h = lax.axis_index("seq"), lax.axis_index("hid")
    c, k = s // G, s % G
    planes = [(h + t) % H for t in range(1, H)]
    places = [(c + t) % L for t in range(1, L)]
    mates = [(k + t) % G for t in range(1, G)]
    piece = w_ref.shape[2]
    loads = []
    for z in range(H):
        for n in range(L * G):
            at = (z * L * G + n) * piece
            copy = pltpu.make_async_copy(
                w_ref.at[n, z], weights.at[at : at + piece], wsem.at[n, z]
            )
            copy.start()
            loads.append(copy)
    greet(
        [{"hid": z} for z in planes]
        + [{"seq": o * G + k} for o in places]
        + [{"seq": c * G + m} for m in mates]
    )
    for copy in loads:
        copy.wait()
    rows, width = x_ref.shape
    sub = BLOCK // 4
    full = width // HD
    for b in range(rows // BLOCK):
        span = slice(b * BLOCK, (b + 1) * BLOCK)
        branch = jnp.dot(a_ref[span, :], weights[...], preferred_element_type=F32)
        value = x_ref[span, :].astype(F32) + ls_ref[...] * branch
        res[span, :] = value
        one = jnp.sum(value, axis=1, keepdims=True)
        two = jnp.sum(value * value, axis=1, keepdims=True)
        for n, column in ((0, one), (1, two)):
            summed = sum(column[q * sub : (q + 1) * sub] for q in range(4))
            stats[h, n, b * sub : (b + 1) * sub, :] = jnp.broadcast_to(summed, (sub, HD))
    sent = []
    for t, z in enumerate(planes):
        copy = remote(stats.at[h], stats.at[h], ssend.at[t], srecv.at[h], {"hid": z})
        copy.start()
        sent.append(copy)
    lanes[...] = jnp.zeros_like(lanes)
    row = lax.broadcasted_iota(jnp.int32, (4 * HD, 4 * HD), 0)
    col = lax.broadcasted_iota(jnp.int32, (4 * HD, 4 * HD), 1)
    place[...] = jnp.where(col == 4 * (row % HD) + lax.div(row, HD), 1.0, 0.0).astype(BF16)
    for j in range(pl.cdiv(width, HD)):
        cols = slice(4 * j * HD, 4 * (j + 1) * HD)
        rest = affine_ref[:, cols]
        total = jnp.zeros_like(rest)
        for _ in range(3):
            term = rest.astype(BF16)
            rest = rest - term.astype(F32)
            total = total + lax.dot_general(
                term, place[...], (((1,), (1,)), ((), ())), preferred_element_type=F32
            )
        affine[:, cols] = total
    for t, z in enumerate(planes):
        remote(stats.at[z], stats.at[z], ssend.at[t], srecv.at[z], {"hid": z}).wait_recv()
    total = stats[0]
    for z in range(1, H):
        total = total + stats[z]
    total = total * (1.0 / (4 * width * H))
    mean = total[0]
    scale = lax.rsqrt(total[1] - mean * mean + 1e-05)
    for b in range(rows // BLOCK):
        part = slice(b * sub, (b + 1) * sub)
        mean_b, scale_b = mean[part, :1], scale[part, :1]
        for q in range(4):
            start = b * BLOCK + q * sub
            value = (res[start : start + sub, :] - mean_b) * scale_b
            for j in range(pl.cdiv(width, HD)):
                size = min(HD, width - j * HD)
                at = (4 * j + q) * HD
                part_value = value[:, j * HD : j * HD + size]
                part_value = part_value * affine[0:1, at : at + size] + affine[1:2, at : at + size]
                lanes[part, at : at + size] = part_value.astype(BF16)
    for j in range(full):
        cols = slice(4 * j * HD, 4 * (j + 1) * HD)
        out[s, :, cols] = jnp.dot(
            lanes[:, cols], place[...], preferred_element_type=F32
        ).astype(BF16)
    if width % HD:
        cols = slice(4 * full * HD, 4 * (full + 1) * HD)
        left = 4 * (width % HD)
        last = jnp.dot(lanes[:, cols], place[...], preferred_element_type=F32)
        out[s, :, 4 * full * HD :] = last[:, :left].astype(BF16)
    for t, o in enumerate(places):
        copy = remote(out.at[s], out.at[s], send1.at[t], recv1.at[c], {"seq": o * G + k})
        copy.start()
        sent.append(copy)

    def share(t, slot, home):
        for u, m in enumerate(mates):
            copy = remote(
                out.at[slot], out.at[slot], send2.at[t, u], recv2.at[home, k], {"seq": c * G + m}
            )
            copy.start()
            sent.append(copy)

    share(0, s, c)
    for t in range(1, L):
        o = (c - t + L) % L
        slot = o * G + k
        remote(out.at[slot], out.at[slot], send1.at[0], recv1.at[o], {"seq": slot}).wait_recv()
        share(t, slot, o)
    for m in mates:
        for t in range(L):
            o = (c + t) % L
            slot = o * G + m
            remote(
                out.at[slot], out.at[slot], send2.at[0, 0], recv2.at[o, m], {"seq": c * G + m}
            ).wait_recv()
    for copy in sent:
        copy.wait_send()


def merge(a, w, x, ls, affine, S, L, H):
    G = S // L
    rows, width = x.shape
    return pl.pallas_call(
        functools.partial(merge_kernel, L, G, H),
        out_shape=jax.ShapeDtypeStruct((S, rows // 4, 4 * width), BF16),
        in_specs=[VMEM, pl.BlockSpec(memory_space=pl.ANY)] + [VMEM] * 3,
        out_specs=VMEM,
        scratch_shapes=[
            pltpu.VMEM((rows, width), F32),
            pltpu.VMEM((H, 2, rows // 4, HD), F32),
            pltpu.VMEM((rows // 4, 4 * HD * pl.cdiv(width, HD)), BF16),
            pltpu.VMEM(affine.shape, F32),
            pltpu.VMEM((4 * HD, 4 * HD), BF16),
            pltpu.VMEM((a.shape[1], width), BF16),
            pltpu.SemaphoreType.DMA((S, H)),
            pltpu.SemaphoreType.DMA((H,)),
            pltpu.SemaphoreType.DMA((H,)),
            pltpu.SemaphoreType.DMA((L,)),
            pltpu.SemaphoreType.DMA((L,)),
            pltpu.SemaphoreType.DMA((L, G)),
            pltpu.SemaphoreType.DMA((L, G)),
        ],
        compiler_params=params(2),
        name="merge_rows",
    )(a, w, x, ls, affine)


def finish_kernel(
    g, H, m_ref, w_ref, slot_ref, bias_ref, text_ref, mask_ref, gain_ref, stream, normed,
    p_ref, parts, rows_out, rows_in, squares, send1, recv1, send2, recv2, send3, recv3,
):
    s, h = lax.axis_index("seq"), lax.axis_index("hid")
    c, k = s // g, s % g
    planes = [(h + t) % H for t in range(1, H)]
    off = c != h
    barrier = pltpu.get_barrier_semaphore()
    for z in planes:
        pl.semaphore_signal(barrier, inc=1, device_id={"hid": z}, device_id_type=MESH)
    for t in range(g):
        j = (k + t) % g
        partner = {"seq": g * h + j, "hid": c}
        if t:
            pl.semaphore_signal(barrier, inc=1, device_id=partner, device_id_type=MESH)
        else:
            @pl.when(off)
            def _():
                pl.semaphore_signal(barrier, inc=1, device_id=partner, device_id_type=MESH)
    pl.semaphore_wait(barrier, len(planes) + g - 1 + off.astype(jnp.int32))

    sent = []
    part_rows = stream.shape[0]
    width = bias_ref.shape[1]
    step_rows = 2 * part_rows if g % 2 == 0 else part_rows
    steps = g * part_rows // step_rows

    def part(j):
        return slice(j * part_rows, (j + 1) * part_rows)

    def first_send(t, z, j):
        return remote(
            p_ref.at[z, part(j)], parts.at[h, part(j)], send1.at[t, j], recv1.at[h, j], {"hid": z}
        )

    def project(t, carry):
        z = (h + 1 + t) % H

        def some(n, inner):
            at = n * step_rows
            base = z * (g * part_rows) + at
            position = base + lax.broadcasted_iota(jnp.int32, (step_rows, 1), 0)
            chosen = jnp.where(position == slot_ref[...], 1.0, 0.0).astype(BF16)
            rows = jnp.dot(chosen, m_ref[...], preferred_element_type=F32).astype(BF16)
            value = jnp.dot(rows, w_ref[...], preferred_element_type=F32).astype(BF16)
            if steps == 1:
                p_ref[z] = value
            else:
                p_ref[z, pl.ds(pl.multiple_of(at, step_rows), step_rows), :] = value
            return inner

        if steps == 1:
            some(0, 0)
        else:
            lax.fori_loop(0, steps, some, 0)

        @pl.when(t < H - 1)
        def _():
            first_send(t, z, 0).start()

        return carry

    lax.fori_loop(0, H, project, 0)
    for j in range(1, g):
        for t, z in enumerate(planes):
            first_send(t, z, j).start()
    for j in range(g):
        span = part(j)
        value = p_ref[h, span, :].astype(F32)
        for t, z in enumerate(planes):
            copy = remote(
                p_ref.at[z, span], parts.at[z, span], send1.at[t, j], recv1.at[z, j], {"hid": z}
            )
            copy.wait_recv()
            sent.append(copy)
            value = value + parts[z, span, :].astype(F32)
        value = value + bias_ref[...]
        value = value * (lax.erf(value * F32(0.7071067811865476)) + 1.0) * 0.5
        rows_out[j] = jnp.where(
            mask_ref[span, :1] > 0.5, value, text_ref[span, :].astype(F32)
        ).astype(BF16)
        away = jnp.logical_or(off, k != j)

        @pl.when(away)
        def _():
            remote(
                rows_out.at[j], rows_in.at[k], send2.at[j], recv2.at[k],
                {"seq": g * h + j, "hid": c},
            ).start()

        @pl.when(jnp.logical_not(away))
        def _():
            rows_in[k] = rows_out[j]

    for j in range(g):
        @pl.when(jnp.logical_or(off, k != j))
        def _():
            copy = remote(
                rows_out.at[j], rows_in.at[j], send2.at[j], recv2.at[j],
                {"seq": g * h + j, "hid": c},
            )
            copy.wait_recv()
            copy.wait_send()

    square = jnp.zeros((part_rows, 1), F32)
    for j in range(g):
        value = rows_in[j]
        stream[:, j * width : (j + 1) * width] = value
        value = value.astype(F32)
        square = square + jnp.sum(value * value, axis=1, keepdims=True)
    squares[h] = jnp.broadcast_to(square, squares.shape[1:])
    for t, z in enumerate(planes):
        copy = remote(squares.at[h], squares.at[h], send3.at[t], recv3.at[h], {"hid": z})
        copy.start()
        sent.append(copy)
    for t, z in enumerate(planes):
        remote(squares.at[z], squares.at[z], send3.at[t], recv3.at[z], {"hid": z}).wait_recv()
    total = squares[0]
    for z in range(1, H):
        total = total + squares[z]
    scale = lax.rsqrt(total * (1.0 / (g * width * H)) + 1e-05)[:, :1]
    normed[...] = (stream[...].astype(F32) * scale * gain_ref[...]).astype(BF16)
    for copy in sent:
        copy.wait_send()


def finish(merged, weight, slots, bias, text, mask, gain, S, H):
    g = S // H
    width = weight.shape[1]
    part_rows = text.shape[0] // g
    shape = jax.ShapeDtypeStruct((part_rows, g * width), BF16)
    return pl.pallas_call(
        functools.partial(finish_kernel, g, H),
        out_shape=(shape, shape),
        in_specs=[VMEM] * 7,
        out_specs=(VMEM, VMEM),
        scratch_shapes=[
            pltpu.VMEM((H, g * part_rows, width), BF16),
            pltpu.VMEM((H, g * part_rows, width), BF16),
            pltpu.VMEM((g, part_rows, width), BF16),
            pltpu.VMEM((g, part_rows, width), BF16),
            pltpu.VMEM((H, part_rows, HD), F32),
            pltpu.SemaphoreType.DMA((H, g)),
            pltpu.SemaphoreType.DMA((H, g)),
            pltpu.SemaphoreType.DMA((g,)),
            pltpu.SemaphoreType.DMA((g,)),
            pltpu.SemaphoreType.DMA((H,)),
            pltpu.SemaphoreType.DMA((H,)),
        ],
        compiler_params=params(3),
        name="finish_rows",
    )(merged, weight, slots, bias, text, mask, gain)


def grouping():
    new = jnp.arange(BLOCK, dtype=jnp.int32)
    half = SIDE // 2
    quarter = BLOCK // 4
    spot, rest = new // quarter, new % quarter
    pair, c2 = rest // half, rest % half
    old = (2 * pair + spot // 2) * SIDE + 2 * c2 + spot % 2
    return (old[:, None] == new[None, :]).astype(BF16)


def per_device(
    patches,
    norm_gain,
    query_weight,
    key_weight,
    value_weight,
    out_weight,
    layer_scale,
    merge_gain,
    merge_bias,
    proj_weight,
    proj_bias,
    text_rows,
    stream_gain,
    tile_counts,
    image_slots,
    text_slots,
):
    S, H = lax.axis_size("seq"), lax.axis_size("hid")
    s, h = lax.axis_index("seq"), lax.axis_index("hid")
    rows, depth = patches.shape
    L = query_weight.shape[1] // HD
    G = S // L
    quarter = depth // H

    head_rows = out_weight.shape[0]
    piece = head_rows // S
    own_rows = lax.dynamic_slice_in_dim(out_weight, s * piece, piece, 0)
    own_rows = jnp.stack(
        [own_rows[:, z * quarter : (z + 1) * quarter] for z in range(H)]
    )

    grouped = jnp.einsum(
        "ij,bjd->bid", grouping(), patches.reshape(rows // BLOCK, BLOCK, depth),
        preferred_element_type=F32,
    ).astype(BF16).reshape(rows, depth)
    tokens_f = grouped.astype(F32)
    normed_in = (
        tokens_f * lax.rsqrt(jnp.mean(tokens_f * tokens_f, -1, keepdims=True) + 1e-06) * norm_gain
    ).astype(BF16)
    queries = (
        jnp.dot(normed_in, query_weight, preferred_element_type=F32) * HD ** (-0.5)
    ).astype(BF16)
    key_rows = jnp.dot(normed_in, key_weight, preferred_element_type=F32).astype(BF16)
    value_rows = jnp.dot(normed_in, value_weight, preferred_element_type=F32).astype(BF16)

    q_all, k_all, v_all, own_cols = exchange(
        queries, key_rows, value_rows, own_rows, S, L, H
    )
    out_cols = lax.all_gather(own_cols, "seq", axis=0, tiled=False)
    tiles = S * rows // TILE
    ends = jnp.cumsum(tile_counts).astype(jnp.int32)
    tile = jnp.arange(tiles, dtype=jnp.int32)
    image = jnp.sum((tile[:, None] >= ends[None, :]).astype(jnp.int32), axis=1)
    bias = jnp.where(image[:, None] == image[None, :], 0.0, -1e30).astype(F32)
    bias = jnp.broadcast_to(bias.reshape(tiles * tiles, 1, 1), (tiles * tiles, 1, HD))
    attended = attend(q_all, k_all, v_all, bias, S, L, H)

    own_tokens = lax.dynamic_slice_in_dim(grouped, h * quarter, quarter, 1)
    own_scale = lax.dynamic_slice_in_dim(layer_scale, h * quarter, quarter, 0)
    padding = 4 * HD * pl.cdiv(quarter, HD) - 4 * quarter
    affine = jnp.pad(jnp.stack([merge_gain, merge_bias]), ((0, 6), (0, padding)))
    merged_normed = merge(
        attended,
        out_cols,
        own_tokens,
        own_scale.reshape(1, quarter),
        affine,
        S,
        L,
        H,
    )
    stream_size = image_slots.shape[0] + text_slots.shape[0]
    share = stream_size // H
    width = proj_weight.shape[1]
    own_positions = h * share + jnp.arange(share, dtype=jnp.int32)
    is_text = own_positions[:, None] == text_slots[None, :]
    text = jnp.dot(is_text.astype(BF16), text_rows, preferred_element_type=F32).astype(BF16)
    is_image = jnp.where(jnp.any(is_text, axis=1, keepdims=True), 0.0, 1.0)
    mask = jnp.broadcast_to(is_image.astype(F32), (share, HD))
    return finish(
        merged_normed.reshape(S * rows // 4, 4 * quarter),
        proj_weight,
        image_slots.reshape(1, image_slots.shape[0]),
        proj_bias.reshape(1, width),
        text,
        mask,
        stream_gain.reshape(1, stream_gain.shape[0]),
        S,
        H,
    )


def solution(mesh):
    return jax.shard_map(
        per_device,
        mesh=mesh,
        in_specs=(
            P("seq", None),
            P(),
            P(None, "hid"),
            P(None, "hid"),
            P(None, "hid"),
            P("hid", None),
            P(),
            P("hid"),
            P("hid"),
            P("hid", "seq"),
            P("seq"),
            P(None, "seq"),
            P("hid"),
            P(),
            P(),
            P(),
        ),
        out_specs=(P("seq", "hid"), P("seq", "hid")),
        check_vma=False,
    )
```
